32 devices in a mesh: grp: 2 (over y), tile: 4 (over z), freq: 4 (over x, core).
Axes of the slice: x: 2, y: 2, z: 4, core: 2. Of those that a mesh axis runs over, the one named last changes fastest.
Arguments:
- sources: bfloat16 [4, 4, 2048, 512], P('freq', 'grp', 'tile'), parts along dimension 1, may hold values from -6 to 6
- v_factors: bfloat16 [4, 4, 2, 4, 112, 512], P('freq', 'tile', None, 'grp'), parts along dimension 3, may hold values from -0.1875 to 0.1875
- u_factors: bfloat16 [4, 4, 4, 112, 1024], P('freq', None, 'grp', None, 'tile'), parts along dimension 2, may hold values from -0.1875 to 0.1875
- tile_ranks: int32 [4, 4, 4], P('freq', 'grp', 'tile'), parts along dimension 1, may hold values from 16 to 112, as said below
- window_bounds: int32 [4, 1024, 512], P('grp', ('tile', 'freq')), parts along dimension 0, may hold values from 0 to 31, as said below
Outputs:
- windowed_traces: float32 [1024, 64, 512], P(('tile', 'freq'), 'grp'), parts along dimension 1
The draws below stay inside these ranges and needn't reach their ends.
There are 2 independent parts, one for each index of `grp`. The reference program is written for one: setup_inputs(seed, part) draws one part's arguments, and reference() takes and returns one part's arrays. A program takes and returns all parts, laid end to end along the dimension named above; each array names one. Nothing has to cross between parts.
Inputs may be any that keep to these rules, and one draw needn't show every extreme that they name: `tile_ranks`: each tile's rank for each frequency; rank slots at or beyond it carry no coefficients. window_bounds[1] - window_bounds[0] lies between 8 and 16 for every receiver and virtual source.
All inputs are finite; a program needn't handle non-finite values.
Results may differ from the reference program's by a relative error of at most 0.0041.
Values may be sent and summed in bfloat16 or wider, within the bound.
A program may use at most 64 MiB of HBM per device.

```python
import math
import jax
import jax.numpy as jnp
from jax import lax

B = 512
RMAX = 112
RMIN = 16
S = 512
NT = 32
FREQ = 4
TC = 4
TR = 2
SRC = 2048
REC = 1024


def draw_tile_ranks(key, part):
    tile_total = FREQ * TR * TC
    drawn_ranks = jax.random.randint(jax.random.fold_in(key, 11), (tile_total,), RMIN, RMAX + 1)
    positions = jax.random.permutation(jax.random.fold_in(key, 12), tile_total)
    flat_index = jnp.arange(tile_total)
    drawn_ranks = jnp.where(flat_index == positions[0], RMAX, drawn_ranks)
    drawn_ranks = jnp.where(flat_index == positions[1], RMIN, drawn_ranks)
    return drawn_ranks.reshape(FREQ, TR, TC).astype(jnp.int32)


def draw_window_bounds(key, part):
    lower_edge = jax.random.randint(jax.random.fold_in(key, 21), (REC, S), 0, NT // 2)
    spread = jax.random.randint(jax.random.fold_in(key, 22), (REC, S), NT // 4, NT // 2 + 1)
    chosen = jax.random.randint(jax.random.fold_in(key, 23), (), 0, REC * S)
    second_spot = (chosen + 1) % (REC * S)
    flat_index = jnp.arange(REC * S).reshape(REC, S)
    lower_edge = jnp.where(flat_index == chosen, NT // 2 - 1, lower_edge)
    spread = jnp.where(flat_index == chosen, NT // 2, spread)
    lower_edge = jnp.where(flat_index == second_spot, 0, lower_edge)
    upper_edge = lower_edge + spread
    return jnp.stack([lower_edge, upper_edge], axis=0).astype(jnp.int32)


def block_scale(own_key, dims, split, smallest, largest):
    factor_of = 1.0
    for position, blocks in split:
        steps = jax.random.uniform(jax.random.fold_in(jax.random.fold_in(own_key, 6), position), (blocks,), jnp.float32, smallest / len(split), largest / len(split))
        factor_of = factor_of * jnp.repeat(jnp.exp(steps), dims[position] // blocks).reshape((-1,) + (1,) * (len(dims) - 1 - position))
    return factor_of


def normal_values(own_key, shape, deviation, reach, split=(), held_as=jnp.bfloat16):
    loudness = block_scale(own_key, shape, split, -0.22, 0.18) if split else 1.0
    values = jax.random.normal(own_key, shape, jnp.float32) * deviation * loudness
    return jnp.minimum(jnp.maximum(values, -reach), reach).astype(held_as)


def setup_inputs(seed: int = 0, part: int = 0) -> dict:
    keys = jax.random.split(jax.random.key(seed), 6)
    part_splits = jax.random.split(jax.random.fold_in(keys[5], part), 6)
    sources = normal_values(part_splits[0], (FREQ, 2, SRC, S), 1.0, 6.0, ((0, 4), (2, 4)))
    v_factors = normal_values(part_splits[1], (FREQ, TC, TR, 2, RMAX, B), (2 * B) ** -0.5, 0.1875, ((0, 4), (1, 4)))
    u_factors = normal_values(part_splits[2], (FREQ, TC, 2, RMAX, REC), (2 * TC * RMAX) ** -0.5, 0.1875, ((0, 4), (4, 4)))
    tile_ranks = draw_tile_ranks(jax.random.fold_in(jax.random.fold_in(keys[5], part), 71), part)
    window_bounds = draw_window_bounds(jax.random.fold_in(jax.random.fold_in(keys[5], part), 71), part)
    return {"sources": sources, "v_factors": v_factors, "u_factors": u_factors, "tile_ranks": tile_ranks, "window_bounds": window_bounds}


first_bin = 2
highest = lax.Precision.HIGHEST

def inverse_tables(count_freq, count_time):
    freq_index = jnp.arange(count_freq, dtype=jnp.int32)[:, None] + first_bin
    time_index = jnp.arange(count_time, dtype=jnp.int32)[None, :]
    phase_step = freq_index * time_index % count_time
    angles = phase_step.astype(jnp.float32) * (2.0 * math.pi / count_time)
    return (jnp.cos(angles), jnp.sin(angles))

def column_coefficients(packed):
    v_column, x_column, rank_column = packed
    products = jnp.einsum('icrb,dbs->icrds', v_column.astype(jnp.float32), x_column.astype(jnp.float32), precision=highest)
    coef_real = products[:, 0, :, 0] - products[:, 1, :, 1]
    coef_imag = products[:, 0, :, 1] + products[:, 1, :, 0]
    slot_index = jnp.arange(RMAX, dtype=jnp.int32)
    live_slots = (slot_index[None, :] < rank_column[:, None])[:, None, :, None]
    stacked = jnp.stack([coef_real, coef_imag], axis=1)
    return jnp.where(live_slots, stacked, jnp.float32(0.0)).astype(jnp.bfloat16)

def row_spectrum(packed):
    u_row, c_row = packed
    products = jnp.einsum('jcrb,jdrs->cbds', u_row.astype(jnp.float32), c_row.astype(jnp.float32), precision=highest)
    real_part = products[0, :, 0] - products[1, :, 1]
    imag_part = products[0, :, 1] + products[1, :, 0]
    return jnp.stack([real_part, imag_part], axis=0).astype(jnp.bfloat16)

def one_frequency(packed):
    v_freq, u_freq, x_freq, rank_freq = packed
    x_columns = x_freq.reshape(2, TC, B, S).transpose(1, 0, 2, 3)
    coefficients = lax.map(column_coefficients, (v_freq, x_columns, rank_freq.T))
    u_rows = u_freq.reshape(TC, 2, RMAX, TR, B).transpose(3, 0, 1, 2, 4)
    spectra = lax.map(row_spectrum, (u_rows, coefficients.transpose(1, 0, 2, 3, 4)))
    return spectra.transpose(1, 0, 2, 3).reshape(2, TR * B, S)

def reference(sources, v_factors, u_factors, tile_ranks, window_bounds):
    spectra = lax.map(one_frequency, (v_factors, u_factors, sources, tile_ranks))
    cosine_table, sine_table = inverse_tables(FREQ, NT)
    widened = spectra.astype(jnp.float32)
    traces = jnp.einsum('frs,fn->rns', widened[:, 0], cosine_table, precision=highest) - jnp.einsum('frs,fn->rns', widened[:, 1], sine_table, precision=highest)
    traces = traces * (1.0 / math.sqrt(FREQ))
    time_index = jnp.arange(NT, dtype=jnp.int32)[None, :, None]
    inside = (time_index >= window_bounds[0][:, None, :]) & (time_index < window_bounds[1][:, None, :])
    return jnp.where(inside, traces, jnp.float32(0.0)).astype(jnp.float32)
```

```python
import functools
import math

import jax
import jax.numpy as jnp
import ml_dtypes
import numpy as np
from jax import lax
from jax.experimental import pallas as pl
from jax.experimental.pallas import tpu as pltpu
from jax.sharding import PartitionSpec as P

NT = 32
FIRST_BIN = 2
LANES = 128
MESH = pl.DeviceIdType.MESH


def repeat(count, body):
    if count <= 4:
        for step in range(count):
            body(step)
    else:

        def one(step, carry):
            body(step)
            return carry

        lax.fori_loop(0, count, one, 0)


def exchange_kernel(
    tiles,
    freqs,
    ranks,
    x_hbm,
    v_hbm,
    u_hbm,
    out,
    x_vm,
    v_vm,
    u_vm,
    own,
    held,
    spec,
    load_sem,
    own_send,
    relay_send,
    coef_recv,
    spec_send,
    spec_recv,
):
    rows = v_vm.shape[0]
    slots = v_vm.shape[2]
    owners = tiles // rows
    chunks = own.shape[0]
    receivers = u_vm.shape[3]
    quarter = receivers // freqs
    me = lax.axis_index("tile")
    my_freq = lax.axis_index("freq")
    my_row = me // owners
    first = my_row * owners
    last = first + owners - 1

    v_load = pltpu.make_async_copy(v_hbm.at[0, 0], v_vm, load_sem.at[0])
    u_load = pltpu.make_async_copy(u_hbm.at[0], u_vm, load_sem.at[1])
    x_loads = []
    for k in range(chunks):
        columns = pl.ds(k * LANES, LANES)
        x_loads.append(
            pltpu.make_async_copy(
                x_hbm.at[0, :, :, columns], x_vm.at[:, :, columns], load_sem.at[2 + k]
            )
        )
    v_load.start()
    for load in x_loads:
        load.start()
    u_load.start()

    barrier = pltpu.get_barrier_semaphore()
    for step in range(1, tiles):
        pl.semaphore_signal(
            barrier,
            inc=1,
            device_id={"tile": lax.rem(me + step, tiles)},
            device_id_type=MESH,
        )
    for step in range(1, freqs):
        pl.semaphore_signal(
            barrier,
            inc=1,
            device_id={"freq": lax.rem(my_freq + step, freqs)},
            device_id_type=MESH,
        )

    def own_copies(k, row):
        low = row * owners
        high = low + owners - 1

        def copy(target, way):
            return pltpu.make_async_remote_copy(
                src_ref=own.at[k, row],
                dst_ref=held.at[k, me],
                send_sem=own_send.at[k, row, way],
                recv_sem=coef_recv.at[k, me],
                device_id={"tile": target},
                device_id_type=MESH,
            )

        upward = copy(jnp.maximum(jnp.minimum(me + 1, tiles - 1), low), 0)
        downward = copy(jnp.minimum(jnp.maximum(me - 1, 0), high), 1)
        return (me < high, upward), (me > low, downward)

    def relay_copy(k, source):
        from_below = source < me
        wanted = jnp.where(from_below, me < last, me > first)
        target = jnp.where(from_below, jnp.minimum(me + 1, tiles - 1), jnp.maximum(me - 1, 0))
        copy = pltpu.make_async_remote_copy(
            src_ref=held.at[k, source],
            dst_ref=held.at[k, source],
            send_sem=relay_send.at[k, source],
            recv_sem=coef_recv.at[k, source],
            device_id={"tile": target},
            device_id_type=MESH,
        )
        return wanted, copy

    def arrival(step):
        below = me
        above = tiles - 1 - me
        below_first = jnp.where(step < below, me - 1 - step, step + 1)
        above_first = jnp.where(step < above, me + 1 + step, me - 1 - (step - above))
        return jnp.where((me - first) * 2 < owners, below_first, above_first)

    def spec_copy(k, step):
        target = lax.rem(my_freq + step, freqs)
        return pltpu.make_async_remote_copy(
            src_ref=spec.at[k, target],
            dst_ref=out.at[my_freq, :, :, pl.ds(k * LANES, LANES)],
            send_sem=spec_send.at[k, step],
            recv_sem=spec_recv.at[k, my_freq],
            device_id={"freq": target},
            device_id_type=MESH,
        )

    def spec_local(k):
        return pltpu.make_async_copy(
            spec.at[k, my_freq],
            out.at[my_freq, :, :, pl.ds(k * LANES, LANES)],
            spec_send.at[k, 0],
        )

    v_load.wait()
    slot_index = lax.broadcasted_iota(jnp.int32, (slots, 2 * LANES), 0)
    for k in range(chunks):
        x_loads[k].wait()
        columns = slice(k * LANES, (k + 1) * LANES)
        x_pair = jnp.concatenate([x_vm[0, :, columns], x_vm[1, :, columns]], axis=1)

        def make_row(row, k=k, x_pair=x_pair):
            products = jnp.dot(
                v_vm[row].reshape(2 * slots, v_vm.shape[3]),
                x_pair,
                preferred_element_type=jnp.float32,
            )
            real = products[:slots, :LANES] - products[slots:, LANES:]
            imag = products[:slots, LANES:] + products[slots:, :LANES]
            pair = jnp.concatenate([real, imag], axis=1)
            live = slot_index < ranks[0, row, 0]
            own[k, row] = jnp.where(live, pair, 0.0).astype(jnp.bfloat16)

        repeat(rows, make_row)
        held[k, me] = own[k, my_row]
        if k == 0:
            pl.semaphore_wait(barrier, tiles - 1 + freqs - 1)

        def send_row(row, k=k):
            for wanted, copy in own_copies(k, row):
                pl.when(wanted)(copy.start)

        repeat(rows, send_row)

    u_load.wait()
    for k in range(chunks):

        def take(step, k=k):
            source = arrival(step)
            wanted, copy = relay_copy(k, source)
            copy.wait_recv()
            pl.when(wanted)(copy.start)

        repeat(tiles - 1, take)
        coef = held[k].reshape(tiles * slots, 2 * LANES)
        contract = (((0,), (0,)), ((), ()))
        by_real = lax.dot_general(
            u_vm[:, 0].reshape(tiles * slots, receivers),
            coef,
            contract,
            preferred_element_type=jnp.float32,
        )
        by_imag = lax.dot_general(
            u_vm[:, 1].reshape(tiles * slots, receivers),
            coef,
            contract,
            preferred_element_type=jnp.float32,
        )
        real = by_real[:, :LANES] - by_imag[:, LANES:]
        imag = by_real[:, LANES:] + by_imag[:, :LANES]
        spec[k, :, 0] = real.astype(jnp.bfloat16).reshape(freqs, quarter, LANES)
        spec[k, :, 1] = imag.astype(jnp.bfloat16).reshape(freqs, quarter, LANES)
        for step in range(1, freqs):
            spec_copy(k, step).start()
        spec_local(k).start()

    for k in range(chunks):

        def drain_row(row, k=k):
            for wanted, copy in own_copies(k, row):
                pl.when(wanted)(copy.wait_send)

        repeat(rows, drain_row)

        def drain_relay(step, k=k):
            wanted, copy = relay_copy(k, arrival(step))
            pl.when(wanted)(copy.wait_send)

        repeat(tiles - 1, drain_relay)
        for step in range(1, freqs):
            spec_copy(k, step).wait_send()
        spec_local(k).wait()
    for k in range(chunks):
        for step in range(1, freqs):
            source = lax.rem(my_freq + step, freqs)
            pltpu.make_async_remote_copy(
                src_ref=spec.at[k, 0],
                dst_ref=out.at[source, :, :, pl.ds(k * LANES, LANES)],
                send_sem=spec_send.at[k, step],
                recv_sem=spec_recv.at[k, source],
                device_id={"freq": source},
                device_id_type=MESH,
            ).wait_recv()


def exchange(ranks, sources, v_factors, u_factors, tiles, freqs):
    rows, _, slots, edge = v_factors.shape[2:]
    receivers = u_factors.shape[4]
    width = sources.shape[3]
    chunks = width // LANES
    quarter = receivers // freqs
    bf16 = jnp.bfloat16
    dma = pltpu.SemaphoreType.DMA
    anywhere = pl.BlockSpec(memory_space=pl.ANY)
    return pl.pallas_call(
        functools.partial(exchange_kernel, tiles, freqs),
        out_shape=jax.ShapeDtypeStruct((freqs, 2, quarter, width), bf16),
        in_specs=[pl.BlockSpec(memory_space=pltpu.SMEM), anywhere, anywhere, anywhere],
        out_specs=anywhere,
        scratch_shapes=[
            pltpu.VMEM(sources.shape[1:], bf16),
            pltpu.VMEM((rows, 2, slots, edge), bf16),
            pltpu.VMEM((tiles, 2, slots, receivers), bf16),
            pltpu.VMEM((chunks, rows, slots, 2 * LANES), bf16),
            pltpu.VMEM((chunks, tiles, slots, 2 * LANES), bf16),
            pltpu.VMEM((chunks, freqs, 2, quarter, LANES), bf16),
            dma((2 + chunks,)),
            dma((chunks, rows, 2)),
            dma((chunks, tiles)),
            dma((chunks, tiles)),
            dma((chunks, freqs)),
            dma((chunks, freqs)),
        ],
        compiler_params=pltpu.CompilerParams(
            collective_id=0, has_side_effects=True, vmem_limit_bytes=56 * 2**20
        ),
        name="exchange",
    )(ranks, sources, v_factors, u_factors)


def block_table(freqs, block):
    steps = (np.arange(freqs)[:, None] + FIRST_BIN) * np.arange(NT)[None, :] % NT
    angles = steps * (2.0 * math.pi / NT)
    table = np.stack([np.cos(angles), -np.sin(angles)], axis=1) / math.sqrt(freqs)
    whole = np.einsum("fcn,rq->rnfcq", table, np.eye(block))
    whole = whole.reshape(block * NT, freqs * 2 * block).astype(np.float32)
    high = whole.astype(ml_dtypes.bfloat16)
    low = (whole - high.astype(np.float32)).astype(ml_dtypes.bfloat16)
    return np.concatenate([high, low], axis=1)


def window_kernel(spec, bounds, table, out):
    block, count, width = out.shape
    depth = table.shape[1] // 2
    part = spec[...].reshape(depth, width)
    stacked = jnp.concatenate([part, part], axis=0)
    traces = jnp.dot(table[...], stacked, preferred_element_type=jnp.float32)
    traces = traces.reshape(block, count, width)
    time_index = lax.broadcasted_iota(jnp.int32, (block, count, width), 1)
    inside = (time_index >= bounds[0][:, None, :]) & (time_index < bounds[1][:, None, :])
    out[...] = jnp.where(inside, traces, 0.0)


def transform(spectra, bounds):
    freqs, _, quarter, width = spectra.shape
    block = 16
    table = jnp.asarray(block_table(freqs, block))
    return pl.pallas_call(
        window_kernel,
        grid=(quarter // block,),
        out_shape=jax.ShapeDtypeStruct((quarter, NT, width), jnp.float32),
        in_specs=[
            pl.BlockSpec((freqs, 2, block, width), lambda r: (0, 0, r, 0)),
            pl.BlockSpec((2, block, width), lambda r: (0, r, 0)),
            pl.BlockSpec(table.shape, lambda r: (0, 0)),
        ],
        out_specs=pl.BlockSpec((block, NT, width), lambda r: (r, 0, 0)),
        compiler_params=pltpu.CompilerParams(vmem_limit_bytes=40 * 2**20),
        name="transform",
    )(spectra, bounds, table)


def solution(mesh):
    tiles = mesh.shape["tile"]
    freqs = mesh.shape["freq"]

    def per_device(sources, v_factors, u_factors, tile_ranks, window_bounds):
        spectra = exchange(tile_ranks, sources, v_factors, u_factors, tiles, freqs)
        return transform(spectra, window_bounds)

    return jax.shard_map(
        per_device,
        mesh=mesh,
        in_specs=(
            P("freq", "grp", "tile", None),
            P("freq", "tile", None, "grp", None, None),
            P("freq", None, "grp", None, "tile"),
            P("freq", "grp", "tile"),
            P("grp", ("tile", "freq"), None),
        ),
        out_specs=P(("tile", "freq"), "grp", None),
        check_vma=False,
    )
```

```python
import functools
import math

import jax
import jax.numpy as jnp
import ml_dtypes
import numpy as np
from jax import lax
from jax.experimental import pallas as pl
from jax.experimental.pallas import tpu as pltpu
from jax.sharding import PartitionSpec as P

NT = 32
FIRST_BIN = 2
LANES = 128
MESH = pl.DeviceIdType.MESH


def repeat(count, body):
    if count <= 4:
        for step in range(count):
            body(step)
    else:

        def one(step, carry):
            body(step)
            return carry

        lax.fori_loop(0, count, one, 0)


def exchange_kernel(
    tiles,
    freqs,
    ranks,
    x_hbm,
    v_hbm,
    u_hbm,
    out,
    x_vm,
    v_vm,
    u_vm,
    own,
    held,
    spec,
    load_sem,
    own_send,
    relay_send,
    coef_recv,
    spec_send,
    spec_recv,
):
    rows = v_vm.shape[0]
    slots = v_vm.shape[2]
    owners = tiles // rows
    chunks = own.shape[0]
    receivers = u_vm.shape[3]
    quarter = receivers // freqs
    me = lax.axis_index("tile")
    my_freq = lax.axis_index("freq")
    my_row = me // owners
    first = my_row * owners
    last = first + owners - 1

    v_load = pltpu.make_async_copy(v_hbm.at[0, 0], v_vm, load_sem.at[0])
    u_load = pltpu.make_async_copy(u_hbm.at[0], u_vm, load_sem.at[1])
    x_loads = []
    for k in range(chunks):
        columns = pl.ds(k * LANES, LANES)
        x_loads.append(
            pltpu.make_async_copy(
                x_hbm.at[0, :, :, columns], x_vm.at[:, :, columns], load_sem.at[2 + k]
            )
        )
    v_load.start()
    for load in x_loads:
        load.start()
    u_load.start()

    barrier = pltpu.get_barrier_semaphore()
    for step in range(1, tiles):
        pl.semaphore_signal(
            barrier,
            inc=1,
            device_id={"tile": lax.rem(me + step, tiles)},
            device_id_type=MESH,
        )
    for step in range(1, freqs):
        pl.semaphore_signal(
            barrier,
            inc=1,
            device_id={"freq": lax.rem(my_freq + step, freqs)},
            device_id_type=MESH,
        )

    def own_copies(k, row):
        low = row * owners
        high = low + owners - 1

        def copy(target, way):
            return pltpu.make_async_remote_copy(
                src_ref=own.at[k, row],
                dst_ref=held.at[k, me],
                send_sem=own_send.at[k, row, way],
                recv_sem=coef_recv.at[k, me],
                device_id={"tile": target},
                device_id_type=MESH,
            )

        upward = copy(jnp.maximum(jnp.minimum(me + 1, tiles - 1), low), 0)
        downward = copy(jnp.minimum(jnp.maximum(me - 1, 0), high), 1)
        return (me < high, upward), (me > low, downward)

    def relay_copy(k, source):
        from_below = source < me
        wanted = jnp.where(from_below, me < last, me > first)
        target = jnp.where(from_below, jnp.minimum(me + 1, tiles - 1), jnp.maximum(me - 1, 0))
        copy = pltpu.make_async_remote_copy(
            src_ref=held.at[k, source],
            dst_ref=held.at[k, source],
            send_sem=relay_send.at[k, source],
            recv_sem=coef_recv.at[k, source],
            device_id={"tile": target},
            device_id_type=MESH,
        )
        return wanted, copy

    def arrival(step):
        below = me
        above = tiles - 1 - me
        below_first = jnp.where(step < below, me - 1 - step, step + 1)
        above_first = jnp.where(step < above, me + 1 + step, me - 1 - (step - above))
        return jnp.where((me - first) * 2 < owners, below_first, above_first)

    def spec_copy(k, step):
        target = lax.rem(my_freq + step, freqs)
        return pltpu.make_async_remote_copy(
            src_ref=spec.at[k, target],
            dst_ref=out.at[my_freq, :, :, pl.ds(k * LANES, LANES)],
            send_sem=spec_send.at[k, step],
            recv_sem=spec_recv.at[k, my_freq],
            device_id={"freq": target},
            device_id_type=MESH,
        )

    def spec_local(k):
        return pltpu.make_async_copy(
            spec.at[k, my_freq],
            out.at[my_freq, :, :, pl.ds(k * LANES, LANES)],
            spec_send.at[k, 0],
        )

    v_load.wait()
    slot_index = lax.broadcasted_iota(jnp.int32, (slots, 2 * LANES), 0)
    for k in range(chunks):
        x_loads[k].wait()
        columns = slice(k * LANES, (k + 1) * LANES)
        x_pair = jnp.concatenate([x_vm[0, :, columns], x_vm[1, :, columns]], axis=1)

        def make_row(row, k=k, x_pair=x_pair):
            products = jnp.dot(
                v_vm[row].reshape(2 * slots, v_vm.shape[3]),
                x_pair,
                preferred_element_type=jnp.float32,
            )
            real = products[:slots, :LANES] - products[slots:, LANES:]
            imag = products[:slots, LANES:] + products[slots:, :LANES]
            pair = jnp.concatenate([real, imag], axis=1)
            live = slot_index < ranks[row]
            own[k, row] = jnp.where(live, pair, 0.0).astype(jnp.bfloat16)

        repeat(rows, make_row)
        held[k, me] = own[k, my_row]
        if k == 0:
            pl.semaphore_wait(barrier, tiles - 1 + freqs - 1)

        def send_row(row, k=k):
            for wanted, copy in own_copies(k, row):
                pl.when(wanted)(copy.start)

        repeat(rows, send_row)

    u_load.wait()
    for k in range(chunks):

        def take(step, k=k):
            source = arrival(step)
            wanted, copy = relay_copy(k, source)
            copy.wait_recv()
            pl.when(wanted)(copy.start)

        repeat(tiles - 1, take)
        coef = held[k].reshape(tiles * slots, 2 * LANES)
        contract = (((0,), (0,)), ((), ()))
        by_real = lax.dot_general(
            u_vm[:, 0].reshape(tiles * slots, receivers),
            coef,
            contract,
            preferred_element_type=jnp.float32,
        )
        by_imag = lax.dot_general(
            u_vm[:, 1].reshape(tiles * slots, receivers),
            coef,
            contract,
            preferred_element_type=jnp.float32,
        )
        real = by_real[:, :LANES] - by_imag[:, LANES:]
        imag = by_real[:, LANES:] + by_imag[:, :LANES]
        spec[k, :, 0] = real.astype(jnp.bfloat16).reshape(freqs, quarter, LANES)
        spec[k, :, 1] = imag.astype(jnp.bfloat16).reshape(freqs, quarter, LANES)
        for step in range(1, freqs):
            spec_copy(k, step).start()
        spec_local(k).start()

    for k in range(chunks):

        def drain_row(row, k=k):
            for wanted, copy in own_copies(k, row):
                pl.when(wanted)(copy.wait_send)

        repeat(rows, drain_row)

        def drain_relay(step, k=k):
            wanted, copy = relay_copy(k, arrival(step))
            pl.when(wanted)(copy.wait_send)

        repeat(tiles - 1, drain_relay)
        for step in range(1, freqs):
            spec_copy(k, step).wait_send()
        spec_local(k).wait()
    for k in range(chunks):
        for step in range(1, freqs):
            source = lax.rem(my_freq + step, freqs)
            pltpu.make_async_remote_copy(
                src_ref=spec.at[k, 0],
                dst_ref=out.at[source, :, :, pl.ds(k * LANES, LANES)],
                send_sem=spec_send.at[k, step],
                recv_sem=spec_recv.at[k, source],
                device_id={"freq": source},
                device_id_type=MESH,
            ).wait_recv()


def exchange(ranks, sources, v_factors, u_factors, tiles, freqs):
    rows, _, slots, edge = v_factors.shape[2:]
    receivers = u_factors.shape[4]
    width = sources.shape[3]
    chunks = width // LANES
    quarter = receivers // freqs
    bf16 = jnp.bfloat16
    dma = pltpu.SemaphoreType.DMA
    anywhere = pl.BlockSpec(memory_space=pl.ANY)
    return pl.pallas_call(
        functools.partial(exchange_kernel, tiles, freqs),
        out_shape=jax.ShapeDtypeStruct((freqs, 2, quarter, width), bf16),
        in_specs=[pl.BlockSpec(memory_space=pltpu.SMEM), anywhere, anywhere, anywhere],
        out_specs=anywhere,
        scratch_shapes=[
            pltpu.VMEM(sources.shape[1:], bf16),
            pltpu.VMEM((rows, 2, slots, edge), bf16),
            pltpu.VMEM((tiles, 2, slots, receivers), bf16),
            pltpu.VMEM((chunks, rows, slots, 2 * LANES), bf16),
            pltpu.VMEM((chunks, tiles, slots, 2 * LANES), bf16),
            pltpu.VMEM((chunks, freqs, 2, quarter, LANES), bf16),
            dma((2 + chunks,)),
            dma((chunks, rows, 2)),
            dma((chunks, tiles)),
            dma((chunks, tiles)),
            dma((chunks, freqs)),
            dma((chunks, freqs)),
        ],
        compiler_params=pltpu.CompilerParams(
            collective_id=0, has_side_effects=True, vmem_limit_bytes=56 * 2**20
        ),
        name="exchange",
    )(ranks.reshape(rows), sources, v_factors, u_factors)


def block_table(freqs, block):
    steps = (np.arange(freqs)[:, None] + FIRST_BIN) * np.arange(NT)[None, :] % NT
    angles = steps * (2.0 * math.pi / NT)
    table = np.stack([np.cos(angles), -np.sin(angles)], axis=1) / math.sqrt(freqs)
    whole = np.einsum("fcn,rq->rnfcq", table, np.eye(block))
    whole = whole.reshape(block * NT, freqs * 2 * block).astype(np.float32)
    high = whole.astype(ml_dtypes.bfloat16)
    low = (whole - high.astype(np.float32)).astype(ml_dtypes.bfloat16)
    return np.concatenate([high, low], axis=1)


def window_kernel(spec, bounds, table, out):
    block, count, width = out.shape
    depth = table.shape[1] // 2
    part = spec[...].reshape(depth, width)
    stacked = jnp.concatenate([part, part], axis=0)
    traces = jnp.dot(table[...], stacked, preferred_element_type=jnp.float32)
    traces = traces.reshape(block, count, width)
    time_index = lax.broadcasted_iota(jnp.int32, (block, count, width), 1)
    inside = (time_index >= bounds[0][:, None, :]) & (time_index < bounds[1][:, None, :])
    out[...] = jnp.where(inside, traces, 0.0)


def transform(spectra, bounds):
    freqs, _, quarter, width = spectra.shape
    block = 16
    table = jnp.asarray(block_table(freqs, block))
    return pl.pallas_call(
        window_kernel,
        grid=(quarter // block,),
        out_shape=jax.ShapeDtypeStruct((quarter, NT, width), jnp.float32),
        in_specs=[
            pl.BlockSpec((freqs, 2, block, width), lambda r: (0, 0, r, 0)),
            pl.BlockSpec((2, block, width), lambda r: (0, r, 0)),
            pl.BlockSpec(table.shape, lambda r: (0, 0)),
        ],
        out_specs=pl.BlockSpec((block, NT, width), lambda r: (r, 0, 0)),
        compiler_params=pltpu.CompilerParams(vmem_limit_bytes=60 * 2**20),
        name="transform",
    )(spectra, bounds, table)


def solution(mesh):
    tiles = mesh.shape["tile"]
    freqs = mesh.shape["freq"]

    def per_device(sources, v_factors, u_factors, tile_ranks, window_bounds):
        spectra = exchange(tile_ranks, sources, v_factors, u_factors, tiles, freqs)
        return transform(spectra, window_bounds)

    return jax.shard_map(
        per_device,
        mesh=mesh,
        in_specs=(
            P("freq", "grp", "tile", None),
            P("freq", "tile", None, "grp", None, None),
            P("freq", None, "grp", None, "tile"),
            P("freq", "grp", "tile"),
            P("grp", ("tile", "freq"), None),
        ),
        out_specs=P(("tile", "freq"), "grp", None),
        check_vma=False,
    )
```

```python
import functools
import math

import jax
import jax.numpy as jnp
import ml_dtypes
import numpy as np
from jax import lax
from jax.experimental import pallas as pl
from jax.experimental.pallas import tpu as pltpu
from jax.sharding import PartitionSpec as P

NT = 32
FIRST_BIN = 2
LANES = 128
MESH = pl.DeviceIdType.MESH


def repeat(count, body):
    if count <= 4:
        for step in range(count):
            body(step)
    else:

        def one(step, carry):
            body(step)
            return carry

        lax.fori_loop(0, count, one, 0)


def exchange_kernel(
    tiles,
    freqs,
    ranks,
    x_hbm,
    v_hbm,
    u_hbm,
    out,
    x_vm,
    v_vm,
    u_vm,
    own,
    held,
    spec,
    load_sem,
    own_send,
    relay_send,
    coef_recv,
    spec_send,
    spec_recv,
):
    rows = v_vm.shape[0]
    slots = v_vm.shape[2]
    assert tiles == 2 * rows
    chunks = own.shape[0]
    receivers = u_vm.shape[3]
    quarter = receivers // freqs
    me = lax.axis_index("tile")
    my_freq = lax.axis_index("freq")
    my_row = me // 2
    partner = me + 1 - 2 * lax.rem(me, 2)
    relayed = me - 1 + 2 * lax.rem(me, 2)
    relaying = (relayed >= 0) & (relayed < tiles)
    relay_source = jnp.clip(relayed, 0, tiles - 1)

    v_load = pltpu.make_async_copy(v_hbm.at[0, 0], v_vm, load_sem.at[0])
    u_load = pltpu.make_async_copy(u_hbm.at[0], u_vm, load_sem.at[1])
    x_loads = []
    for k in range(chunks):
        columns = pl.ds(k * LANES, LANES)
        x_loads.append(
            pltpu.make_async_copy(
                x_hbm.at[0, :, :, columns], x_vm.at[:, :, columns], load_sem.at[2 + k]
            )
        )
    barrier = pltpu.get_barrier_semaphore()
    for step in range(1, tiles):
        pl.semaphore_signal(
            barrier,
            inc=1,
            device_id={"tile": lax.rem(me + step, tiles)},
            device_id_type=MESH,
        )
    for step in range(1, freqs):
        pl.semaphore_signal(
            barrier,
            inc=1,
            device_id={"freq": lax.rem(my_freq + step, freqs)},
            device_id_type=MESH,
        )

    v_load.start()
    for load in x_loads:
        load.start()
    u_load.start()

    def own_copies(k, row):
        low = 2 * row
        high = low + 1

        def copy(target, way):
            return pltpu.make_async_remote_copy(
                src_ref=own.at[k, row],
                dst_ref=held.at[k, me],
                send_sem=own_send.at[k, row, way],
                recv_sem=coef_recv.at[k, me],
                device_id={"tile": target},
                device_id_type=MESH,
            )

        return (
            ((me < low - 1) | (me == low), copy(high, 0)),
            ((me > high + 1) | (me == high), copy(low, 1)),
            (me < low, copy(low, 2)),
            (me > high, copy(high, 3)),
        )

    def relay_copy(k):
        return pltpu.make_async_remote_copy(
            src_ref=held.at[k, relay_source],
            dst_ref=held.at[k, relay_source],
            send_sem=relay_send.at[k],
            recv_sem=coef_recv.at[k, relay_source],
            device_id={"tile": partner},
            device_id_type=MESH,
        )

    def arrived(k, source):
        return pltpu.make_async_remote_copy(
            src_ref=held.at[k, source],
            dst_ref=held.at[k, source],
            send_sem=relay_send.at[k],
            recv_sem=coef_recv.at[k, source],
            device_id={"tile": partner},
            device_id_type=MESH,
        )

    def relay(k):
        @pl.when(relaying)
        def _():
            arrived(k, relay_source).wait_recv()
            relay_copy(k).start()

    def spec_copy(k, step):
        target = lax.rem(my_freq + step, freqs)
        return pltpu.make_async_remote_copy(
            src_ref=spec.at[k, target],
            dst_ref=out.at[my_freq, :, :, pl.ds(k * LANES, LANES)],
            send_sem=spec_send.at[k, step],
            recv_sem=spec_recv.at[k, my_freq],
            device_id={"freq": target},
            device_id_type=MESH,
        )

    def spec_local(k):
        return pltpu.make_async_copy(
            spec.at[k, my_freq],
            out.at[my_freq, :, :, pl.ds(k * LANES, LANES)],
            spec_send.at[k, 0],
        )

    v_load.wait()
    slot_index = lax.broadcasted_iota(jnp.int32, (slots, 2 * LANES), 0)
    for k in range(chunks):
        x_loads[k].wait()
        columns = slice(k * LANES, (k + 1) * LANES)
        x_pair = jnp.concatenate([x_vm[0, :, columns], x_vm[1, :, columns]], axis=1)

        def make_row(row, k=k, x_pair=x_pair):
            products = jnp.dot(
                v_vm[row].reshape(2 * slots, v_vm.shape[3]),
                x_pair,
                preferred_element_type=jnp.float32,
            )
            real = products[:slots, :LANES] - products[slots:, LANES:]
            imag = products[:slots, LANES:] + products[slots:, :LANES]
            pair = jnp.concatenate([real, imag], axis=1)
            live = slot_index < ranks[row]
            own[k, row] = jnp.where(live, pair, 0.0).astype(jnp.bfloat16)

        repeat(rows, make_row)
        held[k, me] = own[k, my_row]
        if k == 0:
            pl.semaphore_wait(barrier, tiles - 1 + freqs - 1)

        def send_row(row, k=k):
            for wanted, copy in own_copies(k, row):
                pl.when(wanted)(copy.start)

        repeat(rows, send_row)
        if k >= 1:
            relay(k - 1)

    relay(chunks - 1)
    u_load.wait()
    for k in range(chunks):

        def take(step, k=k):
            source = lax.rem(me + step + 1, tiles)

            @pl.when(jnp.logical_not(relaying & (source == relay_source)))
            def _():
                arrived(k, source).wait_recv()

        repeat(tiles - 1, take)
        coef = held[k].reshape(tiles * slots, 2 * LANES)
        contract = (((0,), (0,)), ((), ()))
        by_real = lax.dot_general(
            u_vm[:, 0].reshape(tiles * slots, receivers),
            coef,
            contract,
            preferred_element_type=jnp.float32,
        )
        by_imag = lax.dot_general(
            u_vm[:, 1].reshape(tiles * slots, receivers),
            coef,
            contract,
            preferred_element_type=jnp.float32,
        )
        real = by_real[:, :LANES] - by_imag[:, LANES:]
        imag = by_real[:, LANES:] + by_imag[:, :LANES]
        spec[k, :, 0] = real.astype(jnp.bfloat16).reshape(freqs, quarter, LANES)
        spec[k, :, 1] = imag.astype(jnp.bfloat16).reshape(freqs, quarter, LANES)
        for step in sorted(range(1, freqs), key=lambda step: step != freqs // 2):
            spec_copy(k, step).start()
        spec_local(k).start()

    for k in range(chunks):

        def drain_row(row, k=k):
            for wanted, copy in own_copies(k, row):
                pl.when(wanted)(copy.wait_send)

        repeat(rows, drain_row)

        pl.when(relaying)(relay_copy(k).wait_send)
        for step in range(1, freqs):
            spec_copy(k, step).wait_send()
        spec_local(k).wait()
    for k in range(chunks):
        for step in range(1, freqs):
            source = lax.rem(my_freq + step, freqs)
            pltpu.make_async_remote_copy(
                src_ref=spec.at[k, 0],
                dst_ref=out.at[source, :, :, pl.ds(k * LANES, LANES)],
                send_sem=spec_send.at[k, step],
                recv_sem=spec_recv.at[k, source],
                device_id={"freq": source},
                device_id_type=MESH,
            ).wait_recv()


def exchange(ranks, sources, v_factors, u_factors, tiles, freqs):
    rows, _, slots, edge = v_factors.shape[2:]
    receivers = u_factors.shape[4]
    width = sources.shape[3]
    chunks = width // LANES
    quarter = receivers // freqs
    bf16 = jnp.bfloat16
    dma = pltpu.SemaphoreType.DMA
    anywhere = pl.BlockSpec(memory_space=pl.ANY)
    return pl.pallas_call(
        functools.partial(exchange_kernel, tiles, freqs),
        out_shape=jax.ShapeDtypeStruct((freqs, 2, quarter, width), bf16),
        in_specs=[pl.BlockSpec(memory_space=pltpu.SMEM), anywhere, anywhere, anywhere],
        out_specs=anywhere,
        scratch_shapes=[
            pltpu.VMEM(sources.shape[1:], bf16),
            pltpu.VMEM((rows, 2, slots, edge), bf16),
            pltpu.VMEM((tiles, 2, slots, receivers), bf16),
            pltpu.VMEM((chunks, rows, slots, 2 * LANES), bf16),
            pltpu.VMEM((chunks, tiles, slots, 2 * LANES), bf16),
            pltpu.VMEM((chunks, freqs, 2, quarter, LANES), bf16),
            dma((2 + chunks,)),
            dma((chunks, rows, 4)),
            dma((chunks,)),
            dma((chunks, tiles)),
            dma((chunks, freqs)),
            dma((chunks, freqs)),
        ],
        compiler_params=pltpu.CompilerParams(
            collective_id=0, has_side_effects=True, vmem_limit_bytes=56 * 2**20
        ),
        name="exchange",
    )(ranks.reshape(rows), sources, v_factors, u_factors)


def block_table(freqs, block):
    steps = (np.arange(freqs)[:, None] + FIRST_BIN) * np.arange(NT)[None, :] % NT
    angles = steps * (2.0 * math.pi / NT)
    table = np.stack([np.cos(angles), -np.sin(angles)], axis=1) / math.sqrt(freqs)
    whole = np.einsum("fcn,rq->rnfcq", table, np.eye(block))
    whole = whole.reshape(block * NT, freqs * 2 * block).astype(np.float32)
    high = whole.astype(ml_dtypes.bfloat16)
    low = (whole - high.astype(np.float32)).astype(ml_dtypes.bfloat16)
    return np.concatenate([high, low], axis=1)


def window_kernel(
    spec_hbm, bounds_hbm, table_hbm, out_hbm, spec, bounds, table, out, load_sem, store_sem
):
    quarter, count, width = out.shape
    depth = table.shape[1] // 2
    half = table.shape[0] // count // 2
    pieces = quarter // (2 * half)
    table_load = pltpu.make_async_copy(table_hbm, table, load_sem.at[0])
    spec_loads = []
    bounds_loads = []
    for piece in range(pieces):
        part = pl.ds(piece * 2 * half, 2 * half)
        spec_loads.append(
            pltpu.make_async_copy(
                spec_hbm.at[:, :, part], spec.at[:, :, part], load_sem.at[1 + 2 * piece]
            )
        )
        bounds_loads.append(
            pltpu.make_async_copy(
                bounds_hbm.at[:, part], bounds.at[:, part], load_sem.at[2 + 2 * piece]
            )
        )
    spec_loads[0].start()
    table_load.start()
    bounds_loads[0].start()
    for piece in range(1, pieces):
        spec_loads[piece].start()
        bounds_loads[piece].start()
    time_index = lax.broadcasted_iota(jnp.int32, (half, count, width), 1)
    table_load.wait()
    stores = []
    for piece in range(pieces):
        spec_loads[piece].wait()
        bounds_loads[piece].wait()
        base = piece * 2 * half
        block = spec[:, :, base : base + 2 * half, :].reshape(depth, width)
        stacked = jnp.concatenate([block, block], axis=0)
        for side in range(2):
            part = slice(base + side * half, base + (side + 1) * half)
            weights = table[side * half * count : (side + 1) * half * count, :]
            traces = jnp.dot(weights, stacked, preferred_element_type=jnp.float32)
            traces = traces.reshape(half, count, width)
            lower = bounds[0, part, :][:, None, :]
            upper = bounds[1, part, :][:, None, :]
            inside = (time_index >= lower) & (time_index < upper)
            out[part] = jnp.where(inside, traces, 0.0)
            rows = pl.ds(base + side * half, half)
            store = pltpu.make_async_copy(
                out.at[rows], out_hbm.at[rows], store_sem.at[2 * piece + side]
            )
            store.start()
            stores.append(store)
    for store in stores:
        store.wait()


def transform(spectra, bounds):
    freqs, _, quarter, width = spectra.shape
    block = 16
    pieces = quarter // block
    table = jnp.asarray(block_table(freqs, block))
    anywhere = pl.BlockSpec(memory_space=pl.ANY)
    return pl.pallas_call(
        window_kernel,
        out_shape=jax.ShapeDtypeStruct((quarter, NT, width), jnp.float32),
        in_specs=[anywhere] * 3,
        out_specs=anywhere,
        scratch_shapes=[
            pltpu.VMEM(spectra.shape, jnp.bfloat16),
            pltpu.VMEM(bounds.shape, jnp.int32),
            pltpu.VMEM(table.shape, jnp.bfloat16),
            pltpu.VMEM((quarter, NT, width), jnp.float32),
            pltpu.SemaphoreType.DMA((1 + 2 * pieces,)),
            pltpu.SemaphoreType.DMA((2 * pieces,)),
        ],
        compiler_params=pltpu.CompilerParams(vmem_limit_bytes=60 * 2**20),
        name="transform",
    )(spectra, bounds, table)


def solution(mesh):
    tiles = mesh.shape["tile"]
    freqs = mesh.shape["freq"]

    def per_device(sources, v_factors, u_factors, tile_ranks, window_bounds):
        spectra = exchange(tile_ranks, sources, v_factors, u_factors, tiles, freqs)
        return transform(spectra, window_bounds)

    return jax.shard_map(
        per_device,
        mesh=mesh,
        in_specs=(
            P("freq", "grp", "tile", None),
            P("freq", "tile", None, "grp", None, None),
            P("freq", None, "grp", None, "tile"),
            P("freq", "grp", "tile"),
            P("grp", ("tile", "freq"), None),
        ),
        out_specs=P(("tile", "freq"), "grp", None),
        check_vma=False,
    )
```

```python
import functools
import math

import jax
import jax.numpy as jnp
import ml_dtypes
import numpy as np
from jax import lax
from jax.experimental import pallas as pl
from jax.experimental.pallas import tpu as pltpu
from jax.sharding import PartitionSpec as P

NT = 32
FIRST_BIN = 2
LANES = 128
MESH = pl.DeviceIdType.MESH


def repeat(count, body):
    if count <= 4:
        for step in range(count):
            body(step)
    else:

        def one(step, carry):
            body(step)
            return carry

        lax.fori_loop(0, count, one, 0)


def exchange_kernel(
    tiles,
    freqs,
    ranks,
    x_hbm,
    v_hbm,
    u_hbm,
    out,
    x_vm,
    v_vm,
    u_vm,
    own,
    held,
    u_turned,
    spec,
    load_sem,
    own_send,
    relay_send,
    coef_recv,
    spec_send,
    spec_recv,
    ready,
):
    rows = v_vm.shape[0]
    slots = v_vm.shape[2]
    owners = tiles // rows
    chunks = own.shape[0]
    receivers = u_vm.shape[3]
    quarter = receivers // freqs
    me = lax.axis_index("tile")
    my_freq = lax.axis_index("freq")
    my_row = me // owners
    first = my_row * owners
    last = first + owners - 1

    v_load = pltpu.make_async_copy(v_hbm.at[0, 0], v_vm, load_sem.at[0])
    u_load = pltpu.make_async_copy(u_hbm.at[0], u_vm, load_sem.at[1])
    x_loads = []
    for k in range(chunks):
        columns = pl.ds(k * LANES, LANES)
        x_loads.append(
            pltpu.make_async_copy(
                x_hbm.at[0, :, :, columns], x_vm.at[:, :, columns], load_sem.at[2 + k]
            )
        )
    barrier = pltpu.get_barrier_semaphore()
    def greet(semaphore, axis, place, size, way):
        for step in range(1, size):
            target = place + way * step

            @pl.when((target >= 0) & (target < size))
            def _(target=target):
                pl.semaphore_signal(
                    semaphore,
                    inc=1,
                    device_id={axis: jnp.clip(target, 0, size - 1)},
                    device_id_type=MESH,
                )

    greet(barrier, "tile", me, tiles, 1)
    greet(barrier, "freq", my_freq, freqs, 1)

    v_load.start()
    for load in x_loads:
        load.start()
    u_load.start()

    def own_copies(k, row):
        low = row * owners
        high = low + owners - 1

        def copy(target, way):
            return pltpu.make_async_remote_copy(
                src_ref=own.at[k, row],
                dst_ref=held.at[k, me],
                send_sem=own_send.at[k, row, way],
                recv_sem=coef_recv.at[k, me],
                device_id={"tile": target},
                device_id_type=MESH,
            )

        upward = copy(jnp.maximum(jnp.minimum(me + 1, tiles - 1), low), 0)
        downward = copy(jnp.minimum(jnp.maximum(me - 1, 0), high), 1)
        return (me < high, upward), (me > low, downward)

    def relay_copy(k, source):
        from_below = source < me
        wanted = jnp.where(from_below, me < last, me > first)
        target = jnp.where(from_below, jnp.minimum(me + 1, tiles - 1), jnp.maximum(me - 1, 0))
        copy = pltpu.make_async_remote_copy(
            src_ref=held.at[k, source],
            dst_ref=held.at[k, source],
            send_sem=relay_send.at[k, source],
            recv_sem=coef_recv.at[k, source],
            device_id={"tile": target},
            device_id_type=MESH,
        )
        return wanted, copy

    def arrival(step):
        below = me
        above = tiles - 1 - me
        below_first = jnp.where(step < below, me - 1 - step, step + 1)
        above_first = jnp.where(step < above, me + 1 + step, me - 1 - (step - above))
        return jnp.where((me - first) * 2 < owners, below_first, above_first)

    def spec_copy(k, step):
        target = lax.rem(my_freq + step, freqs)
        return pltpu.make_async_remote_copy(
            src_ref=spec.at[k, target],
            dst_ref=out.at[my_freq, :, :, pl.ds(k * LANES, LANES)],
            send_sem=spec_send.at[k, step],
            recv_sem=spec_recv.at[k, my_freq],
            device_id={"freq": target},
            device_id_type=MESH,
        )

    def spec_local(k):
        return pltpu.make_async_copy(
            spec.at[k, my_freq],
            out.at[my_freq, :, :, pl.ds(k * LANES, LANES)],
            spec_send.at[k, 0],
        )

    early = min(2, chunks)
    order = sorted(range(freqs), key=lambda step: (step == 0, step != freqs // 2, step))

    def send(k, way):
        def send_row(row):
            wanted, copy = own_copies(k, row)[way]
            pl.when(wanted)(copy.start)

        repeat(rows, send_row)

    v_load.wait()
    slot_index = lax.broadcasted_iota(jnp.int32, (slots, 2 * LANES), 0)
    for k in range(chunks):
        x_loads[k].wait()
        columns = slice(k * LANES, (k + 1) * LANES)
        x_pair = jnp.concatenate([x_vm[0, :, columns], x_vm[1, :, columns]], axis=1)

        def make_row(row, k=k, x_pair=x_pair):
            products = jnp.dot(
                v_vm[row].reshape(2 * slots, v_vm.shape[3]),
                x_pair,
                preferred_element_type=jnp.float32,
            )
            real = products[:slots, :LANES] - products[slots:, LANES:]
            imag = products[:slots, LANES:] + products[slots:, :LANES]
            pair = jnp.concatenate([real, imag], axis=1)
            live = slot_index < ranks[row]
            own[k, row] = jnp.where(live, pair, 0.0).astype(jnp.bfloat16)

        repeat(rows, make_row)
        held[k, me] = own[k, my_row]
        if k == 0:

            @pl.when(me + my_freq > 0)
            def _():
                pl.semaphore_wait(barrier, me + my_freq)

            greet(ready.at[0], "tile", me, tiles, -1)
            greet(ready.at[1], "freq", my_freq, freqs, -1)
        send(k, 1)
        if k == early - 1:

            @pl.when(me < tiles - 1)
            def _():
                pl.semaphore_wait(ready.at[0], tiles - 1 - me)

            for earlier in range(early):
                send(earlier, 0)
        elif k >= early:
            send(k, 0)

    u_load.wait()
    for part in range(2):
        turned = u_vm[:, part].reshape(tiles * slots, receivers).T
        u_turned[:, pl.ds(part * quarter, quarter)] = turned.reshape(
            freqs, quarter, tiles * slots
        )

    @pl.when(my_freq < freqs - 1)
    def _():
        pl.semaphore_wait(ready.at[1], freqs - 1 - my_freq)

    for k in range(chunks):

        def take(step, k=k):
            source = arrival(step)
            wanted, copy = relay_copy(k, source)
            copy.wait_recv()
            pl.when(wanted)(copy.start)

        repeat(tiles - 1, take)
        coef = held[k].reshape(tiles * slots, 2 * LANES)
        for step in order:
            target = lax.rem(my_freq + step, freqs)
            products = jnp.dot(u_turned[target], coef, preferred_element_type=jnp.float32)
            real = products[:quarter, :LANES] - products[quarter:, LANES:]
            imag = products[:quarter, LANES:] + products[quarter:, :LANES]
            spec[k, target, 0] = real.astype(jnp.bfloat16)
            spec[k, target, 1] = imag.astype(jnp.bfloat16)
            if step > 0:
                spec_copy(k, step).start()
        spec_local(k).start()

    for k in range(chunks):

        def drain_row(row, k=k):
            for wanted, copy in own_copies(k, row):
                pl.when(wanted)(copy.wait_send)

        repeat(rows, drain_row)

        def drain_relay(step, k=k):
            wanted, copy = relay_copy(k, arrival(step))
            pl.when(wanted)(copy.wait_send)

        repeat(tiles - 1, drain_relay)
        for step in range(1, freqs):
            spec_copy(k, step).wait_send()
        spec_local(k).wait()
    for k in range(chunks):
        for step in range(1, freqs):
            source = lax.rem(my_freq + step, freqs)
            pltpu.make_async_remote_copy(
                src_ref=spec.at[k, 0],
                dst_ref=out.at[source, :, :, pl.ds(k * LANES, LANES)],
                send_sem=spec_send.at[k, step],
                recv_sem=spec_recv.at[k, source],
                device_id={"freq": source},
                device_id_type=MESH,
            ).wait_recv()


def exchange(ranks, sources, v_factors, u_factors, tiles, freqs):
    rows, _, slots, edge = v_factors.shape[2:]
    receivers = u_factors.shape[4]
    width = sources.shape[3]
    chunks = width // LANES
    quarter = receivers // freqs
    bf16 = jnp.bfloat16
    dma = pltpu.SemaphoreType.DMA
    anywhere = pl.BlockSpec(memory_space=pl.ANY)
    return pl.pallas_call(
        functools.partial(exchange_kernel, tiles, freqs),
        out_shape=jax.ShapeDtypeStruct((freqs, 2, quarter, width), bf16),
        in_specs=[pl.BlockSpec(memory_space=pltpu.SMEM), anywhere, anywhere, anywhere],
        out_specs=anywhere,
        scratch_shapes=[
            pltpu.VMEM(sources.shape[1:], bf16),
            pltpu.VMEM((rows, 2, slots, edge), bf16),
            pltpu.VMEM((tiles, 2, slots, receivers), bf16),
            pltpu.VMEM((chunks, rows, slots, 2 * LANES), bf16),
            pltpu.VMEM((chunks, tiles, slots, 2 * LANES), bf16),
            pltpu.VMEM((freqs, 2 * quarter, tiles * slots), bf16),
            pltpu.VMEM((chunks, freqs, 2, quarter, LANES), bf16),
            dma((2 + chunks,)),
            dma((chunks, rows, 2)),
            dma((chunks, tiles)),
            dma((chunks, tiles)),
            dma((chunks, freqs)),
            dma((chunks, freqs)),
            pltpu.SemaphoreType.REGULAR((2,)),
        ],
        compiler_params=pltpu.CompilerParams(
            collective_id=0, has_side_effects=True, vmem_limit_bytes=56 * 2**20
        ),
        name="exchange",
    )(ranks.reshape(rows), sources, v_factors, u_factors)


def block_table(freqs, block):
    steps = (np.arange(freqs)[:, None] + FIRST_BIN) * np.arange(NT)[None, :] % NT
    angles = steps * (2.0 * math.pi / NT)
    table = np.stack([np.cos(angles), -np.sin(angles)], axis=1) / math.sqrt(freqs)
    whole = np.einsum("fcn,rq->rnfcq", table, np.eye(block))
    whole = whole.reshape(block * NT, freqs * 2 * block).astype(np.float32)
    high = whole.astype(ml_dtypes.bfloat16)
    low = (whole - high.astype(np.float32)).astype(ml_dtypes.bfloat16)
    return np.concatenate([high, low], axis=1)


def window_kernel(
    spec_hbm, bounds_hbm, table_hbm, out_hbm, spec, bounds, table, out, load_sem, store_sem
):
    quarter, count, width = out.shape
    depth = table.shape[1] // 2
    half = table.shape[0] // count // 2
    pieces = quarter // (2 * half)
    table_load = pltpu.make_async_copy(table_hbm, table, load_sem.at[0])
    spec_loads = []
    bounds_loads = []
    for piece in range(pieces):
        part = pl.ds(piece * 2 * half, 2 * half)
        spec_loads.append(
            pltpu.make_async_copy(
                spec_hbm.at[:, :, part], spec.at[:, :, part], load_sem.at[1 + 2 * piece]
            )
        )
        bounds_loads.append(
            pltpu.make_async_copy(
                bounds_hbm.at[:, part], bounds.at[:, part], load_sem.at[2 + 2 * piece]
            )
        )
    spec_loads[0].start()
    table_load.start()
    bounds_loads[0].start()
    for piece in range(1, pieces):
        spec_loads[piece].start()
        bounds_loads[piece].start()
    time_index = lax.broadcasted_iota(jnp.int32, (half, count, width), 1)
    table_load.wait()
    stores = []
    for piece in range(pieces):
        spec_loads[piece].wait()
        bounds_loads[piece].wait()
        base = piece * 2 * half
        block = spec[:, :, base : base + 2 * half, :].reshape(depth, width)
        stacked = jnp.concatenate([block, block], axis=0)
        for side in range(2):
            part = slice(base + side * half, base + (side + 1) * half)
            weights = table[side * half * count : (side + 1) * half * count, :]
            traces = jnp.dot(weights, stacked, preferred_element_type=jnp.float32)
            traces = traces.reshape(half, count, width)
            lower = bounds[0, part, :][:, None, :]
            upper = bounds[1, part, :][:, None, :]
            inside = (time_index >= lower) & (time_index < upper)
            out[part] = jnp.where(inside, traces, 0.0)
            rows = pl.ds(base + side * half, half)
            store = pltpu.make_async_copy(
                out.at[rows], out_hbm.at[rows], store_sem.at[2 * piece + side]
            )
            store.start()
            stores.append(store)
    for store in stores:
        store.wait()


def transform(spectra, bounds):
    freqs, _, quarter, width = spectra.shape
    block = 16
    pieces = quarter // block
    table = jnp.asarray(block_table(freqs, block))
    anywhere = pl.BlockSpec(memory_space=pl.ANY)
    return pl.pallas_call(
        window_kernel,
        out_shape=jax.ShapeDtypeStruct((quarter, NT, width), jnp.float32),
        in_specs=[anywhere] * 3,
        out_specs=anywhere,
        scratch_shapes=[
            pltpu.VMEM(spectra.shape, jnp.bfloat16),
            pltpu.VMEM(bounds.shape, jnp.int32),
            pltpu.VMEM(table.shape, jnp.bfloat16),
            pltpu.VMEM((quarter, NT, width), jnp.float32),
            pltpu.SemaphoreType.DMA((1 + 2 * pieces,)),
            pltpu.SemaphoreType.DMA((2 * pieces,)),
        ],
        compiler_params=pltpu.CompilerParams(vmem_limit_bytes=60 * 2**20),
        name="transform",
    )(spectra, bounds, table)


def solution(mesh):
    tiles = mesh.shape["tile"]
    freqs = mesh.shape["freq"]

    def per_device(sources, v_factors, u_factors, tile_ranks, window_bounds):
        spectra = exchange(tile_ranks, sources, v_factors, u_factors, tiles, freqs)
        return transform(spectra, window_bounds)

    return jax.shard_map(
        per_device,
        mesh=mesh,
        in_specs=(
            P("freq", "grp", "tile", None),
            P("freq", "tile", None, "grp", None, None),
            P("freq", None, "grp", None, "tile"),
            P("freq", "grp", "tile"),
            P("grp", ("tile", "freq"), None),
        ),
        out_specs=P(("tile", "freq"), "grp", None),
        check_vma=False,
    )
```

```python
import functools
import math

import jax
import jax.numpy as jnp
import ml_dtypes
import numpy as np
from jax import lax
from jax.experimental import pallas as pl
from jax.experimental.pallas import tpu as pltpu
from jax.sharding import PartitionSpec as P

NT = 32
FIRST_BIN = 2
LANES = 128
BLOCK = 16
MESH = pl.DeviceIdType.MESH


def repeat(count, body):
    if count <= 4:
        for step in range(count):
            body(step)
    else:

        def one(step, carry):
            body(step)
            return carry

        lax.fori_loop(0, count, one, 0)


def exchange_kernel(
    tiles,
    freqs,
    ranks,
    x_hbm,
    v_hbm,
    u_hbm,
    bounds_hbm,
    table_hbm,
    out,
    bounds_out,
    table_out,
    x_vm,
    v_vm,
    u_vm,
    own,
    held,
    u_turned,
    spec,
    load_sem,
    own_send,
    relay_send,
    coef_recv,
    spec_send,
    spec_recv,
    ready,
):
    rows = v_vm.shape[0]
    slots = v_vm.shape[2]
    owners = tiles // rows
    chunks = own.shape[0]
    receivers = u_vm.shape[3]
    quarter = receivers // freqs
    me = lax.axis_index("tile")
    my_freq = lax.axis_index("freq")
    my_row = me // owners
    first = my_row * owners
    last = first + owners - 1

    v_load = pltpu.make_async_copy(v_hbm.at[0, 0], v_vm, load_sem.at[0])
    u_load = pltpu.make_async_copy(u_hbm.at[0], u_vm, load_sem.at[1])
    bounds_load = pltpu.make_async_copy(bounds_hbm, bounds_out, load_sem.at[2 + chunks])
    table_load = pltpu.make_async_copy(table_hbm, table_out, load_sem.at[3 + chunks])
    x_loads = []
    for k in range(chunks):
        columns = pl.ds(k * LANES, LANES)
        x_loads.append(
            pltpu.make_async_copy(
                x_hbm.at[0, :, :, columns], x_vm.at[:, :, columns], load_sem.at[2 + k]
            )
        )
    barrier = pltpu.get_barrier_semaphore()
    def greet(semaphore, axis, place, size, way):
        for step in range(1, size):
            target = place + way * step

            @pl.when((target >= 0) & (target < size))
            def _(target=target):
                pl.semaphore_signal(
                    semaphore,
                    inc=1,
                    device_id={axis: jnp.clip(target, 0, size - 1)},
                    device_id_type=MESH,
                )

    greet(barrier, "tile", me, tiles, 1)
    greet(barrier, "freq", my_freq, freqs, 1)

    v_load.start()
    for load in x_loads:
        load.start()
    u_load.start()
    bounds_load.start()
    table_load.start()

    def own_copies(k, row):
        low = row * owners
        high = low + owners - 1

        def copy(target, way):
            return pltpu.make_async_remote_copy(
                src_ref=own.at[k, row],
                dst_ref=held.at[k, me],
                send_sem=own_send.at[k, row, way],
                recv_sem=coef_recv.at[k, me],
                device_id={"tile": target},
                device_id_type=MESH,
            )

        upward = copy(jnp.maximum(jnp.minimum(me + 1, tiles - 1), low), 0)
        downward = copy(jnp.minimum(jnp.maximum(me - 1, 0), high), 1)
        return (me < high, upward), (me > low, downward)

    def relay_copy(k, source):
        from_below = source < me
        wanted = jnp.where(from_below, me < last, me > first)
        target = jnp.where(from_below, jnp.minimum(me + 1, tiles - 1), jnp.maximum(me - 1, 0))
        copy = pltpu.make_async_remote_copy(
            src_ref=held.at[k, source],
            dst_ref=held.at[k, source],
            send_sem=relay_send.at[k, source],
            recv_sem=coef_recv.at[k, source],
            device_id={"tile": target},
            device_id_type=MESH,
        )
        return wanted, copy

    def arrival(step):
        below = me
        above = tiles - 1 - me
        below_first = jnp.where(step < below, me - 1 - step, step + 1)
        above_first = jnp.where(step < above, me + 1 + step, me - 1 - (step - above))
        return jnp.where((me - first) * 2 < owners, below_first, above_first)

    def spec_copy(k, step):
        target = lax.rem(my_freq + step, freqs)
        return pltpu.make_async_remote_copy(
            src_ref=spec.at[k, target],
            dst_ref=out.at[my_freq, :, :, pl.ds(k * LANES, LANES)],
            send_sem=spec_send.at[k, step],
            recv_sem=spec_recv.at[k, my_freq],
            device_id={"freq": target},
            device_id_type=MESH,
        )

    def spec_local(k):
        return pltpu.make_async_copy(
            spec.at[k, my_freq],
            out.at[my_freq, :, :, pl.ds(k * LANES, LANES)],
            spec_send.at[k, 0],
        )

    early = min(2, chunks)
    order = sorted(range(freqs), key=lambda step: (step == 0, step != freqs // 2, step))

    def send(k, way):
        def send_row(row):
            wanted, copy = own_copies(k, row)[way]
            pl.when(wanted)(copy.start)

        repeat(rows, send_row)

    v_load.wait()
    slot_index = lax.broadcasted_iota(jnp.int32, (slots, 2 * LANES), 0)
    for k in range(chunks):
        x_loads[k].wait()
        columns = slice(k * LANES, (k + 1) * LANES)
        x_pair = jnp.concatenate([x_vm[0, :, columns], x_vm[1, :, columns]], axis=1)

        def make_row(row, k=k, x_pair=x_pair):
            products = jnp.dot(
                v_vm[row].reshape(2 * slots, v_vm.shape[3]),
                x_pair,
                preferred_element_type=jnp.float32,
            )
            real = products[:slots, :LANES] - products[slots:, LANES:]
            imag = products[:slots, LANES:] + products[slots:, :LANES]
            pair = jnp.concatenate([real, imag], axis=1)
            live = slot_index < ranks[row]
            own[k, row] = jnp.where(live, pair, 0.0).astype(jnp.bfloat16)

        repeat(rows, make_row)
        held[k, me] = own[k, my_row]
        if k == 0:

            @pl.when(me + my_freq > 0)
            def _():
                pl.semaphore_wait(barrier, me + my_freq)

            greet(ready.at[0], "tile", me, tiles, -1)
            greet(ready.at[1], "freq", my_freq, freqs, -1)
        send(k, 1)
        if k == early - 1:

            @pl.when(me < tiles - 1)
            def _():
                pl.semaphore_wait(ready.at[0], tiles - 1 - me)

            for earlier in range(early):
                send(earlier, 0)
        elif k >= early:
            send(k, 0)

    u_load.wait()
    for part in range(2):
        turned = u_vm[:, part].reshape(tiles * slots, receivers).T
        u_turned[:, pl.ds(part * quarter, quarter)] = turned.reshape(
            freqs, quarter, tiles * slots
        )

    @pl.when(my_freq < freqs - 1)
    def _():
        pl.semaphore_wait(ready.at[1], freqs - 1 - my_freq)

    for k in range(chunks):

        def take(step, k=k):
            source = arrival(step)
            wanted, copy = relay_copy(k, source)
            copy.wait_recv()
            pl.when(wanted)(copy.start)

        repeat(tiles - 1, take)
        coef = held[k].reshape(tiles * slots, 2 * LANES)
        for step in order:
            target = lax.rem(my_freq + step, freqs)
            products = jnp.dot(u_turned[target], coef, preferred_element_type=jnp.float32)
            real = products[:quarter, :LANES] - products[quarter:, LANES:]
            imag = products[:quarter, LANES:] + products[quarter:, :LANES]
            spec[k, target, 0] = real.astype(jnp.bfloat16)
            spec[k, target, 1] = imag.astype(jnp.bfloat16)
            if step > 0:
                spec_copy(k, step).start()
        spec_local(k).start()

    bounds_load.wait()
    table_load.wait()
    for k in range(chunks):

        def drain_row(row, k=k):
            for wanted, copy in own_copies(k, row):
                pl.when(wanted)(copy.wait_send)

        repeat(rows, drain_row)

        def drain_relay(step, k=k):
            wanted, copy = relay_copy(k, arrival(step))
            pl.when(wanted)(copy.wait_send)

        repeat(tiles - 1, drain_relay)
        for step in range(1, freqs):
            spec_copy(k, step).wait_send()
        spec_local(k).wait()
    for k in range(chunks):
        for step in range(1, freqs):
            source = lax.rem(my_freq + step, freqs)
            pltpu.make_async_remote_copy(
                src_ref=spec.at[k, 0],
                dst_ref=out.at[source, :, :, pl.ds(k * LANES, LANES)],
                send_sem=spec_send.at[k, step],
                recv_sem=spec_recv.at[k, source],
                device_id={"freq": source},
                device_id_type=MESH,
            ).wait_recv()


def exchange(ranks, sources, v_factors, u_factors, bounds, table, tiles, freqs):
    rows, _, slots, edge = v_factors.shape[2:]
    receivers = u_factors.shape[4]
    width = sources.shape[3]
    chunks = width // LANES
    quarter = receivers // freqs
    bf16 = jnp.bfloat16
    dma = pltpu.SemaphoreType.DMA
    anywhere = pl.BlockSpec(memory_space=pl.ANY)
    within = pl.BlockSpec(memory_space=pltpu.VMEM)
    return pl.pallas_call(
        functools.partial(exchange_kernel, tiles, freqs),
        out_shape=(
            pltpu.VMEM((freqs, 2, quarter, width), bf16),
            pltpu.VMEM(bounds.shape, bounds.dtype),
            pltpu.VMEM(table.shape, table.dtype),
        ),
        in_specs=[pl.BlockSpec(memory_space=pltpu.SMEM)] + [anywhere] * 5,
        out_specs=(within, within, within),
        scratch_shapes=[
            pltpu.VMEM(sources.shape[1:], bf16),
            pltpu.VMEM((rows, 2, slots, edge), bf16),
            pltpu.VMEM((tiles, 2, slots, receivers), bf16),
            pltpu.VMEM((chunks, rows, slots, 2 * LANES), bf16),
            pltpu.VMEM((chunks, tiles, slots, 2 * LANES), bf16),
            pltpu.VMEM((freqs, 2 * quarter, tiles * slots), bf16),
            pltpu.VMEM((chunks, freqs, 2, quarter, LANES), bf16),
            dma((4 + chunks,)),
            dma((chunks, rows, 2)),
            dma((chunks, tiles)),
            dma((chunks, tiles)),
            dma((chunks, freqs)),
            dma((chunks, freqs)),
            pltpu.SemaphoreType.REGULAR((2,)),
        ],
        compiler_params=pltpu.CompilerParams(
            collective_id=0, has_side_effects=True, vmem_limit_bytes=56 * 2**20
        ),
        name="exchange",
    )(ranks.reshape(rows), sources, v_factors, u_factors, bounds, table)


def block_table(freqs, block):
    steps = (np.arange(freqs)[:, None] + FIRST_BIN) * np.arange(NT)[None, :] % NT
    angles = steps * (2.0 * math.pi / NT)
    table = np.stack([np.cos(angles), -np.sin(angles)], axis=1) / math.sqrt(freqs)
    whole = np.einsum("fcn,rq->rnfcq", table, np.eye(block))
    whole = whole.reshape(block * NT, freqs * 2 * block).astype(np.float32)
    high = whole.astype(ml_dtypes.bfloat16)
    low = (whole - high.astype(np.float32)).astype(ml_dtypes.bfloat16)
    return np.concatenate([high, low], axis=1)


def window_kernel(spec, bounds, table, out_hbm, out, store_sem):
    quarter, count, width = out.shape
    depth = table.shape[1] // 2
    half = table.shape[0] // count // 2
    pieces = quarter // (2 * half)
    time_index = lax.broadcasted_iota(jnp.int32, (half, count, width), 1)
    stores = []
    for piece in range(pieces):
        base = piece * 2 * half
        block = spec[:, :, base : base + 2 * half, :].reshape(depth, width)
        stacked = jnp.concatenate([block, block], axis=0)
        for side in range(2):
            part = slice(base + side * half, base + (side + 1) * half)
            weights = table[side * half * count : (side + 1) * half * count, :]
            traces = jnp.dot(weights, stacked, preferred_element_type=jnp.float32)
            traces = traces.reshape(half, count, width)
            lower = bounds[0, part, :][:, None, :]
            upper = bounds[1, part, :][:, None, :]
            inside = (time_index >= lower) & (time_index < upper)
            out[part] = jnp.where(inside, traces, 0.0)
            rows = pl.ds(base + side * half, half)
            store = pltpu.make_async_copy(
                out.at[rows], out_hbm.at[rows], store_sem.at[2 * piece + side]
            )
            store.start()
            stores.append(store)
    for store in stores:
        store.wait()


def transform(spectra, bounds, table):
    quarter, width = bounds.shape[1:]
    stores = 2 * quarter // BLOCK
    return pl.pallas_call(
        window_kernel,
        out_shape=jax.ShapeDtypeStruct((quarter, NT, width), jnp.float32),
        in_specs=[pl.BlockSpec(memory_space=pltpu.VMEM)] * 3,
        out_specs=pl.BlockSpec(memory_space=pl.ANY),
        scratch_shapes=[
            pltpu.VMEM((quarter, NT, width), jnp.float32),
            pltpu.SemaphoreType.DMA((stores,)),
        ],
        compiler_params=pltpu.CompilerParams(vmem_limit_bytes=24 * 2**20),
        name="transform",
    )(spectra, bounds, table)


def solution(mesh):
    tiles = mesh.shape["tile"]
    freqs = mesh.shape["freq"]

    def per_device(sources, v_factors, u_factors, tile_ranks, window_bounds):
        table = jnp.asarray(block_table(freqs, BLOCK))
        handed = exchange(
            tile_ranks, sources, v_factors, u_factors, window_bounds, table, tiles, freqs
        )
        return transform(*handed)

    return jax.shard_map(
        per_device,
        mesh=mesh,
        in_specs=(
            P("freq", "grp", "tile", None),
            P("freq", "tile", None, "grp", None, None),
            P("freq", None, "grp", None, "tile"),
            P("freq", "grp", "tile"),
            P("grp", ("tile", "freq"), None),
        ),
        out_specs=P(("tile", "freq"), "grp", None),
        check_vma=False,
    )
```

```python
import functools
import math

import jax
import jax.numpy as jnp
import ml_dtypes
import numpy as np
from jax import lax
from jax.experimental import pallas as pl
from jax.experimental.pallas import tpu as pltpu
from jax.sharding import PartitionSpec as P

NT = 32
FIRST_BIN = 2
LANES = 128
BLOCK = 16
MESH = pl.DeviceIdType.MESH


def repeat(count, body):
    if count <= 4:
        for step in range(count):
            body(step)
    else:

        def one(step, carry):
            body(step)
            return carry

        lax.fori_loop(0, count, one, 0)


def exchange_kernel(
    tiles,
    freqs,
    ranks,
    x_hbm,
    v_hbm,
    u_hbm,
    bounds_hbm,
    table_hbm,
    out,
    bounds_out,
    table_out,
    x_vm,
    v_vm,
    u_vm,
    own,
    held,
    u_turned,
    spec,
    load_sem,
    own_send,
    relay_send,
    coef_recv,
    spec_send,
    spec_recv,
    ready,
):
    rows = v_vm.shape[0]
    slots = v_vm.shape[2]
    owners = tiles // rows
    chunks = own.shape[0]
    receivers = u_vm.shape[3]
    quarter = receivers // freqs
    me = lax.axis_index("tile")
    my_freq = lax.axis_index("freq")
    my_row = me // owners
    first = my_row * owners
    last = first + owners - 1

    v_load = pltpu.make_async_copy(v_hbm.at[0, 0], v_vm, load_sem.at[0])
    u_load = pltpu.make_async_copy(u_hbm.at[0], u_vm, load_sem.at[1])
    bounds_load = pltpu.make_async_copy(bounds_hbm, bounds_out, load_sem.at[2 + chunks])
    table_load = pltpu.make_async_copy(table_hbm, table_out, load_sem.at[3 + chunks])
    x_loads = []
    for k in range(chunks):
        columns = pl.ds(k * LANES, LANES)
        x_loads.append(
            pltpu.make_async_copy(
                x_hbm.at[0, :, :, columns], x_vm.at[:, :, columns], load_sem.at[2 + k]
            )
        )
    barrier = pltpu.get_barrier_semaphore()
    def greet(semaphore, axis, place, size, way):
        for step in range(1, size):
            target = place + way * step

            @pl.when((target >= 0) & (target < size))
            def _(target=target):
                pl.semaphore_signal(
                    semaphore,
                    inc=1,
                    device_id={axis: jnp.clip(target, 0, size - 1)},
                    device_id_type=MESH,
                )

    greet(barrier, "tile", me, tiles, 1)
    greet(barrier, "freq", my_freq, freqs, 1)

    v_load.start()
    for load in x_loads:
        load.start()
    u_load.start()
    bounds_load.start()
    table_load.start()

    def own_copies(k, row):
        low = row * owners
        high = low + owners - 1

        def copy(target, way):
            return pltpu.make_async_remote_copy(
                src_ref=own.at[k, row],
                dst_ref=held.at[k, me],
                send_sem=own_send.at[k, row, way],
                recv_sem=coef_recv.at[k, me],
                device_id={"tile": target},
                device_id_type=MESH,
            )

        upward = copy(jnp.maximum(jnp.minimum(me + 1, tiles - 1), low), 0)
        downward = copy(jnp.minimum(jnp.maximum(me - 1, 0), high), 1)
        return (me < high, upward), (me > low, downward)

    def relay_copy(k, source):
        from_below = source < me
        wanted = jnp.where(from_below, me < last, me > first)
        target = jnp.where(from_below, jnp.minimum(me + 1, tiles - 1), jnp.maximum(me - 1, 0))
        copy = pltpu.make_async_remote_copy(
            src_ref=held.at[k, source],
            dst_ref=held.at[k, source],
            send_sem=relay_send.at[k, source],
            recv_sem=coef_recv.at[k, source],
            device_id={"tile": target},
            device_id_type=MESH,
        )
        return wanted, copy

    def arrival(step):
        below = me
        above = tiles - 1 - me
        below_first = jnp.where(step < below, me - 1 - step, step + 1)
        above_first = jnp.where(step < above, me + 1 + step, me - 1 - (step - above))
        return jnp.where((me - first) * 2 < owners, below_first, above_first)

    def spec_copy(k, step):
        target = lax.rem(my_freq + step, freqs)
        return pltpu.make_async_remote_copy(
            src_ref=spec.at[k, target],
            dst_ref=out.at[my_freq, :, :, pl.ds(k * LANES, LANES)],
            send_sem=spec_send.at[k, step],
            recv_sem=spec_recv.at[k, my_freq],
            device_id={"freq": target},
            device_id_type=MESH,
        )

    def spec_local(k):
        return pltpu.make_async_copy(
            spec.at[k, my_freq],
            out.at[my_freq, :, :, pl.ds(k * LANES, LANES)],
            spec_send.at[k, 0],
        )

    early = min(2, chunks)
    order = sorted(range(freqs), key=lambda step: (step == 0, step != freqs // 2, step))

    def send(k, way):
        def send_row(row):
            wanted, copy = own_copies(k, row)[way]
            pl.when(wanted)(copy.start)

        repeat(rows, send_row)

    v_load.wait()
    slot_index = lax.broadcasted_iota(jnp.int32, (slots, 2 * LANES), 0)
    for k in range(chunks):
        x_loads[k].wait()
        columns = slice(k * LANES, (k + 1) * LANES)
        x_pair = jnp.concatenate([x_vm[0, :, columns], x_vm[1, :, columns]], axis=1)

        def make_row(row, k=k, x_pair=x_pair):
            products = jnp.dot(
                v_vm[row].reshape(2 * slots, v_vm.shape[3]),
                x_pair,
                preferred_element_type=jnp.float32,
            )
            real = products[:slots, :LANES] - products[slots:, LANES:]
            imag = products[:slots, LANES:] + products[slots:, :LANES]
            pair = jnp.concatenate([real, imag], axis=1)
            live = slot_index < ranks[row]
            own[k, row] = jnp.where(live, pair, 0.0).astype(jnp.bfloat16)

        repeat(rows, make_row)
        held[k, me] = own[k, my_row]
        if k == 0:

            @pl.when(me + my_freq > 0)
            def _():
                pl.semaphore_wait(barrier, me + my_freq)

            greet(ready.at[0], "tile", me, tiles, -1)
            greet(ready.at[1], "freq", my_freq, freqs, -1)
        send(k, 1)
        if k == early - 1:

            @pl.when(me < tiles - 1)
            def _():
                pl.semaphore_wait(ready.at[0], tiles - 1 - me)

            for earlier in range(early):
                send(earlier, 0)
        elif k >= early:
            send(k, 0)

    u_load.wait()
    for part in range(2):
        turned = u_vm[:, part].reshape(tiles * slots, receivers).T
        u_turned[:, pl.ds(part * quarter, quarter)] = turned.reshape(
            freqs, quarter, tiles * slots
        )

    @pl.when(my_freq < freqs - 1)
    def _():
        pl.semaphore_wait(ready.at[1], freqs - 1 - my_freq)

    def relay(k):
        def one(step):
            wanted, copy = relay_copy(k, arrival(step))

            @pl.when(wanted)
            def _():
                copy.wait_recv()
                copy.start()

        repeat(tiles - 1, one)

    relay(0)
    for k in range(chunks):
        if k + 1 < chunks:
            relay(k + 1)

        def take(step, k=k):
            wanted, copy = relay_copy(k, arrival(step))
            pl.when(jnp.logical_not(wanted))(copy.wait_recv)

        repeat(tiles - 1, take)
        coef = held[k].reshape(tiles * slots, 2 * LANES)
        for step in order:
            target = lax.rem(my_freq + step, freqs)
            products = jnp.dot(u_turned[target], coef, preferred_element_type=jnp.float32)
            real = products[:quarter, :LANES] - products[quarter:, LANES:]
            imag = products[:quarter, LANES:] + products[quarter:, :LANES]
            spec[k, target, 0] = real.astype(jnp.bfloat16)
            spec[k, target, 1] = imag.astype(jnp.bfloat16)
            if step > 0:
                spec_copy(k, step).start()
        spec_local(k).start()

    bounds_load.wait()
    table_load.wait()
    for k in range(chunks):

        def drain_row(row, k=k):
            for wanted, copy in own_copies(k, row):
                pl.when(wanted)(copy.wait_send)

        repeat(rows, drain_row)

        def drain_relay(step, k=k):
            wanted, copy = relay_copy(k, arrival(step))
            pl.when(wanted)(copy.wait_send)

        repeat(tiles - 1, drain_relay)
        for step in range(1, freqs):
            spec_copy(k, step).wait_send()
        spec_local(k).wait()
    for k in range(chunks):
        for step in range(1, freqs):
            source = lax.rem(my_freq + step, freqs)
            pltpu.make_async_remote_copy(
                src_ref=spec.at[k, 0],
                dst_ref=out.at[source, :, :, pl.ds(k * LANES, LANES)],
                send_sem=spec_send.at[k, step],
                recv_sem=spec_recv.at[k, source],
                device_id={"freq": source},
                device_id_type=MESH,
            ).wait_recv()


def exchange(ranks, sources, v_factors, u_factors, bounds, table, tiles, freqs):
    rows, _, slots, edge = v_factors.shape[2:]
    receivers = u_factors.shape[4]
    width = sources.shape[3]
    chunks = width // LANES
    quarter = receivers // freqs
    bf16 = jnp.bfloat16
    dma = pltpu.SemaphoreType.DMA
    anywhere = pl.BlockSpec(memory_space=pl.ANY)
    within = pl.BlockSpec(memory_space=pltpu.VMEM)
    return pl.pallas_call(
        functools.partial(exchange_kernel, tiles, freqs),
        out_shape=(
            pltpu.VMEM((freqs, 2, quarter, width), bf16),
            pltpu.VMEM(bounds.shape, bounds.dtype),
            pltpu.VMEM(table.shape, table.dtype),
        ),
        in_specs=[pl.BlockSpec(memory_space=pltpu.SMEM)] + [anywhere] * 5,
        out_specs=(within, within, within),
        scratch_shapes=[
            pltpu.VMEM(sources.shape[1:], bf16),
            pltpu.VMEM((rows, 2, slots, edge), bf16),
            pltpu.VMEM((tiles, 2, slots, receivers), bf16),
            pltpu.VMEM((chunks, rows, slots, 2 * LANES), bf16),
            pltpu.VMEM((chunks, tiles, slots, 2 * LANES), bf16),
            pltpu.VMEM((freqs, 2 * quarter, tiles * slots), bf16),
            pltpu.VMEM((chunks, freqs, 2, quarter, LANES), bf16),
            dma((4 + chunks,)),
            dma((chunks, rows, 2)),
            dma((chunks, tiles)),
            dma((chunks, tiles)),
            dma((chunks, freqs)),
            dma((chunks, freqs)),
            pltpu.SemaphoreType.REGULAR((2,)),
        ],
        compiler_params=pltpu.CompilerParams(
            collective_id=0, has_side_effects=True, vmem_limit_bytes=56 * 2**20
        ),
        name="exchange",
    )(ranks.reshape(rows), sources, v_factors, u_factors, bounds, table)


def block_table(freqs, block):
    steps = (np.arange(freqs)[:, None] + FIRST_BIN) * np.arange(NT)[None, :] % NT
    angles = steps * (2.0 * math.pi / NT)
    table = np.stack([np.cos(angles), -np.sin(angles)], axis=1) / math.sqrt(freqs)
    whole = np.einsum("fcn,rq->rnfcq", table, np.eye(block))
    whole = whole.reshape(block * NT, freqs * 2 * block).astype(np.float32)
    high = whole.astype(ml_dtypes.bfloat16)
    low = (whole - high.astype(np.float32)).astype(ml_dtypes.bfloat16)
    return np.concatenate([high, low], axis=1)


def window_kernel(spec, bounds, table, out_hbm, out, store_sem):
    quarter, count, width = out.shape
    depth = table.shape[1] // 2
    half = table.shape[0] // count // 2
    pieces = quarter // (2 * half)
    time_index = lax.broadcasted_iota(jnp.int32, (half, count, width), 1)
    stores = []
    for piece in range(pieces):
        base = piece * 2 * half
        block = spec[:, :, base : base + 2 * half, :].reshape(depth, width)
        stacked = jnp.concatenate([block, block], axis=0)
        for side in range(2):
            part = slice(base + side * half, base + (side + 1) * half)
            weights = table[side * half * count : (side + 1) * half * count, :]
            traces = jnp.dot(weights, stacked, preferred_element_type=jnp.float32)
            traces = traces.reshape(half, count, width)
            lower = bounds[0, part, :][:, None, :]
            upper = bounds[1, part, :][:, None, :]
            inside = (time_index >= lower) & (time_index < upper)
            out[part] = jnp.where(inside, traces, 0.0)
            rows = pl.ds(base + side * half, half)
            store = pltpu.make_async_copy(
                out.at[rows], out_hbm.at[rows], store_sem.at[2 * piece + side]
            )
            store.start()
            stores.append(store)
    for store in stores:
        store.wait()


def transform(spectra, bounds, table):
    quarter, width = bounds.shape[1:]
    stores = 2 * quarter // BLOCK
    return pl.pallas_call(
        window_kernel,
        out_shape=jax.ShapeDtypeStruct((quarter, NT, width), jnp.float32),
        in_specs=[pl.BlockSpec(memory_space=pltpu.VMEM)] * 3,
        out_specs=pl.BlockSpec(memory_space=pl.ANY),
        scratch_shapes=[
            pltpu.VMEM((quarter, NT, width), jnp.float32),
            pltpu.SemaphoreType.DMA((stores,)),
        ],
        compiler_params=pltpu.CompilerParams(vmem_limit_bytes=24 * 2**20),
        name="transform",
    )(spectra, bounds, table)


def solution(mesh):
    tiles = mesh.shape["tile"]
    freqs = mesh.shape["freq"]

    def per_device(sources, v_factors, u_factors, tile_ranks, window_bounds):
        table = jnp.asarray(block_table(freqs, BLOCK))
        handed = exchange(
            tile_ranks, sources, v_factors, u_factors, window_bounds, table, tiles, freqs
        )
        return transform(*handed)

    return jax.shard_map(
        per_device,
        mesh=mesh,
        in_specs=(
            P("freq", "grp", "tile", None),
            P("freq", "tile", None, "grp", None, None),
            P("freq", None, "grp", None, "tile"),
            P("freq", "grp", "tile"),
            P("grp", ("tile", "freq"), None),
        ),
        out_specs=P(("tile", "freq"), "grp", None),
        check_vma=False,
    )
```

```python
import functools
import math

import jax
import jax.numpy as jnp
import ml_dtypes
import numpy as np
from jax import lax
from jax.experimental import pallas as pl
from jax.experimental.pallas import tpu as pltpu
from jax.sharding import PartitionSpec as P

NT = 32
FIRST_BIN = 2
LANES = 128
BLOCK = 16
MESH = pl.DeviceIdType.MESH


def repeat(count, body):
    if count <= 4:
        for step in range(count):
            body(step)
    else:

        def one(step, carry):
            body(step)
            return carry

        lax.fori_loop(0, count, one, 0)


def exchange_kernel(
    tiles,
    freqs,
    ranks,
    x_hbm,
    v_hbm,
    u_hbm,
    bounds_hbm,
    table_hbm,
    out,
    bounds_out,
    table_out,
    x_vm,
    v_vm,
    u_vm,
    own,
    held,
    u_turned,
    spec,
    load_sem,
    own_send,
    relay_send,
    coef_recv,
    spec_send,
    spec_recv,
    ready,
):
    rows = v_vm.shape[0]
    slots = v_vm.shape[2]
    owners = tiles // rows
    chunks = own.shape[0]
    receivers = u_vm.shape[3]
    quarter = receivers // freqs
    me = lax.axis_index("tile")
    my_freq = lax.axis_index("freq")
    my_row = me // owners
    first = my_row * owners
    last = first + owners - 1

    v_load = pltpu.make_async_copy(v_hbm.at[0, 0], v_vm, load_sem.at[0])
    u_load = pltpu.make_async_copy(u_hbm.at[0], u_vm, load_sem.at[1])
    bounds_load = pltpu.make_async_copy(bounds_hbm, bounds_out, load_sem.at[2 + chunks])
    table_load = pltpu.make_async_copy(table_hbm, table_out, load_sem.at[3 + chunks])
    x_loads = []
    for k in range(chunks):
        columns = pl.ds(k * LANES, LANES)
        x_loads.append(
            pltpu.make_async_copy(
                x_hbm.at[0, :, :, columns], x_vm.at[:, :, columns], load_sem.at[2 + k]
            )
        )
    barrier = pltpu.get_barrier_semaphore()
    def greet(semaphore, axis, place, size, way):
        for step in range(1, size):
            target = place + way * step

            @pl.when((target >= 0) & (target < size))
            def _(target=target):
                pl.semaphore_signal(
                    semaphore,
                    inc=1,
                    device_id={axis: jnp.clip(target, 0, size - 1)},
                    device_id_type=MESH,
                )

    greet(barrier, "tile", me, tiles, 1)
    greet(barrier, "freq", my_freq, freqs, 1)

    v_load.start()
    x_loads[0].start()

    def own_copies(k, row):
        low = row * owners
        high = low + owners - 1

        def copy(target, way):
            return pltpu.make_async_remote_copy(
                src_ref=own.at[k, row],
                dst_ref=held.at[k, me],
                send_sem=own_send.at[k, row, way],
                recv_sem=coef_recv.at[k, me],
                device_id={"tile": target},
                device_id_type=MESH,
            )

        upward = copy(jnp.maximum(jnp.minimum(me + 1, tiles - 1), low), 0)
        downward = copy(jnp.minimum(jnp.maximum(me - 1, 0), high), 1)
        return (me < high, upward), (me > low, downward)

    def relay_copy(k, source):
        from_below = source < me
        wanted = jnp.where(from_below, me < last, me > first)
        target = jnp.where(from_below, jnp.minimum(me + 1, tiles - 1), jnp.maximum(me - 1, 0))
        copy = pltpu.make_async_remote_copy(
            src_ref=held.at[k, source],
            dst_ref=held.at[k, source],
            send_sem=relay_send.at[k, source],
            recv_sem=coef_recv.at[k, source],
            device_id={"tile": target},
            device_id_type=MESH,
        )
        return wanted, copy

    def arrival(step):
        below = me
        above = tiles - 1 - me
        below_first = jnp.where(step < below, me - 1 - step, step + 1)
        above_first = jnp.where(step < above, me + 1 + step, me - 1 - (step - above))
        return jnp.where((me - first) * 2 < owners, below_first, above_first)

    def spec_copy(k, step):
        target = lax.rem(my_freq + step, freqs)
        return pltpu.make_async_remote_copy(
            src_ref=spec.at[k, target],
            dst_ref=out.at[my_freq, :, :, pl.ds(k * LANES, LANES)],
            send_sem=spec_send.at[k, step],
            recv_sem=spec_recv.at[k, my_freq],
            device_id={"freq": target},
            device_id_type=MESH,
        )

    def spec_local(k):
        return pltpu.make_async_copy(
            spec.at[k, my_freq],
            out.at[my_freq, :, :, pl.ds(k * LANES, LANES)],
            spec_send.at[k, 0],
        )

    early = min(2, chunks)
    order = sorted(range(freqs), key=lambda step: (step == 0, step != freqs // 2, step))

    def send(k, way):
        def send_row(row):
            wanted, copy = own_copies(k, row)[way]
            pl.when(wanted)(copy.start)

        repeat(rows, send_row)

    v_load.wait()
    slot_index = lax.broadcasted_iota(jnp.int32, (slots, 2 * LANES), 0)
    for k in range(chunks):
        x_loads[k].wait()
        if k == 0:
            for load in x_loads[1:]:
                load.start()
        columns = slice(k * LANES, (k + 1) * LANES)
        x_pair = jnp.concatenate([x_vm[0, :, columns], x_vm[1, :, columns]], axis=1)

        def make_row(row, k=k, x_pair=x_pair):
            products = jnp.dot(
                v_vm[row].reshape(2 * slots, v_vm.shape[3]),
                x_pair,
                preferred_element_type=jnp.float32,
            )
            real = products[:slots, :LANES] - products[slots:, LANES:]
            imag = products[:slots, LANES:] + products[slots:, :LANES]
            pair = jnp.concatenate([real, imag], axis=1)
            live = slot_index < ranks[row]
            own[k, row] = jnp.where(live, pair, 0.0).astype(jnp.bfloat16)

        repeat(rows, make_row)
        held[k, me] = own[k, my_row]
        if k == 0:

            @pl.when(me + my_freq > 0)
            def _():
                pl.semaphore_wait(barrier, me + my_freq)

            greet(ready.at[0], "tile", me, tiles, -1)
            greet(ready.at[1], "freq", my_freq, freqs, -1)
            send(k, 1)
            u_load.start()
            bounds_load.start()
            table_load.start()
        else:
            send(k, 1)
        if k == early - 1:

            @pl.when(me < tiles - 1)
            def _():
                pl.semaphore_wait(ready.at[0], tiles - 1 - me)

            for earlier in range(early):
                send(earlier, 0)
        elif k >= early:
            send(k, 0)

    u_load.wait()
    for part in range(2):
        turned = u_vm[:, part].reshape(tiles * slots, receivers).T
        u_turned[:, pl.ds(part * quarter, quarter)] = turned.reshape(
            freqs, quarter, tiles * slots
        )

    @pl.when(my_freq < freqs - 1)
    def _():
        pl.semaphore_wait(ready.at[1], freqs - 1 - my_freq)

    for k in range(chunks):

        def take(step, k=k):
            source = arrival(step)
            wanted, copy = relay_copy(k, source)
            copy.wait_recv()
            pl.when(wanted)(copy.start)

        repeat(tiles - 1, take)
        coef = held[k].reshape(tiles * slots, 2 * LANES)
        for step in order:
            target = lax.rem(my_freq + step, freqs)
            products = jnp.dot(u_turned[target], coef, preferred_element_type=jnp.float32)
            real = products[:quarter, :LANES] - products[quarter:, LANES:]
            imag = products[:quarter, LANES:] + products[quarter:, :LANES]
            spec[k, target, 0] = real.astype(jnp.bfloat16)
            spec[k, target, 1] = imag.astype(jnp.bfloat16)
            if step > 0:
                spec_copy(k, step).start()
        spec_local(k).start()

    bounds_load.wait()
    table_load.wait()
    for k in range(chunks):

        def drain_row(row, k=k):
            for wanted, copy in own_copies(k, row):
                pl.when(wanted)(copy.wait_send)

        repeat(rows, drain_row)

        def drain_relay(step, k=k):
            wanted, copy = relay_copy(k, arrival(step))
            pl.when(wanted)(copy.wait_send)

        repeat(tiles - 1, drain_relay)
        for step in range(1, freqs):
            spec_copy(k, step).wait_send()
        spec_local(k).wait()
    for k in range(chunks):
        for step in range(1, freqs):
            source = lax.rem(my_freq + step, freqs)
            pltpu.make_async_remote_copy(
                src_ref=spec.at[k, 0],
                dst_ref=out.at[source, :, :, pl.ds(k * LANES, LANES)],
                send_sem=spec_send.at[k, step],
                recv_sem=spec_recv.at[k, source],
                device_id={"freq": source},
                device_id_type=MESH,
            ).wait_recv()


def exchange(ranks, sources, v_factors, u_factors, bounds, table, tiles, freqs):
    rows, _, slots, edge = v_factors.shape[2:]
    receivers = u_factors.shape[4]
    width = sources.shape[3]
    chunks = width // LANES
    quarter = receivers // freqs
    bf16 = jnp.bfloat16
    dma = pltpu.SemaphoreType.DMA
    anywhere = pl.BlockSpec(memory_space=pl.ANY)
    within = pl.BlockSpec(memory_space=pltpu.VMEM)
    return pl.pallas_call(
        functools.partial(exchange_kernel, tiles, freqs),
        out_shape=(
            pltpu.VMEM((freqs, 2, quarter, width), bf16),
            pltpu.VMEM(bounds.shape, bounds.dtype),
            pltpu.VMEM(table.shape, table.dtype),
        ),
        in_specs=[pl.BlockSpec(memory_space=pltpu.SMEM)] + [anywhere] * 5,
        out_specs=(within, within, within),
        scratch_shapes=[
            pltpu.VMEM(sources.shape[1:], bf16),
            pltpu.VMEM((rows, 2, slots, edge), bf16),
            pltpu.VMEM((tiles, 2, slots, receivers), bf16),
            pltpu.VMEM((chunks, rows, slots, 2 * LANES), bf16),
            pltpu.VMEM((chunks, tiles, slots, 2 * LANES), bf16),
            pltpu.VMEM((freqs, 2 * quarter, tiles * slots), bf16),
            pltpu.VMEM((chunks, freqs, 2, quarter, LANES), bf16),
            dma((4 + chunks,)),
            dma((chunks, rows, 2)),
            dma((chunks, tiles)),
            dma((chunks, tiles)),
            dma((chunks, freqs)),
            dma((chunks, freqs)),
            pltpu.SemaphoreType.REGULAR((2,)),
        ],
        compiler_params=pltpu.CompilerParams(
            collective_id=0, has_side_effects=True, vmem_limit_bytes=56 * 2**20
        ),
        name="exchange",
    )(ranks.reshape(rows), sources, v_factors, u_factors, bounds, table)


def block_table(freqs, block):
    steps = (np.arange(freqs)[:, None] + FIRST_BIN) * np.arange(NT)[None, :] % NT
    angles = steps * (2.0 * math.pi / NT)
    table = np.stack([np.cos(angles), -np.sin(angles)], axis=1) / math.sqrt(freqs)
    whole = np.einsum("fcn,rq->rnfcq", table, np.eye(block))
    whole = whole.reshape(block * NT, freqs * 2 * block).astype(np.float32)
    high = whole.astype(ml_dtypes.bfloat16)
    low = (whole - high.astype(np.float32)).astype(ml_dtypes.bfloat16)
    return np.concatenate([high, low], axis=1)


def window_kernel(spec, bounds, table, out_hbm, out, store_sem):
    quarter, count, width = out.shape
    depth = table.shape[1] // 2
    half = table.shape[0] // count // 2
    pieces = quarter // (2 * half)
    time_index = lax.broadcasted_iota(jnp.int32, (half, count, width), 1)
    stores = []
    for piece in range(pieces):
        base = piece * 2 * half
        block = spec[:, :, base : base + 2 * half, :].reshape(depth, width)
        stacked = jnp.concatenate([block, block], axis=0)
        for side in range(2):
            part = slice(base + side * half, base + (side + 1) * half)
            weights = table[side * half * count : (side + 1) * half * count, :]
            traces = jnp.dot(weights, stacked, preferred_element_type=jnp.float32)
            traces = traces.reshape(half, count, width)
            lower = bounds[0, part, :][:, None, :]
            upper = bounds[1, part, :][:, None, :]
            inside = (time_index >= lower) & (time_index < upper)
            out[part] = jnp.where(inside, traces, 0.0)
            rows = pl.ds(base + side * half, half)
            store = pltpu.make_async_copy(
                out.at[rows], out_hbm.at[rows], store_sem.at[2 * piece + side]
            )
            store.start()
            stores.append(store)
    for store in stores:
        store.wait()


def transform(spectra, bounds, table):
    quarter, width = bounds.shape[1:]
    stores = 2 * quarter // BLOCK
    return pl.pallas_call(
        window_kernel,
        out_shape=jax.ShapeDtypeStruct((quarter, NT, width), jnp.float32),
        in_specs=[pl.BlockSpec(memory_space=pltpu.VMEM)] * 3,
        out_specs=pl.BlockSpec(memory_space=pl.ANY),
        scratch_shapes=[
            pltpu.VMEM((quarter, NT, width), jnp.float32),
            pltpu.SemaphoreType.DMA((stores,)),
        ],
        compiler_params=pltpu.CompilerParams(vmem_limit_bytes=24 * 2**20),
        name="transform",
    )(spectra, bounds, table)


def solution(mesh):
    tiles = mesh.shape["tile"]
    freqs = mesh.shape["freq"]

    def per_device(sources, v_factors, u_factors, tile_ranks, window_bounds):
        table = jnp.asarray(block_table(freqs, BLOCK))
        handed = exchange(
            tile_ranks, sources, v_factors, u_factors, window_bounds, table, tiles, freqs
        )
        return transform(*handed)

    return jax.shard_map(
        per_device,
        mesh=mesh,
        in_specs=(
            P("freq", "grp", "tile", None),
            P("freq", "tile", None, "grp", None, None),
            P("freq", None, "grp", None, "tile"),
            P("freq", "grp", "tile"),
            P("grp", ("tile", "freq"), None),
        ),
        out_specs=P(("tile", "freq"), "grp", None),
        check_vma=False,
    )
```

```python
import functools
import math

import jax
import jax.numpy as jnp
import ml_dtypes
import numpy as np
from jax import lax
from jax.experimental import pallas as pl
from jax.experimental.pallas import tpu as pltpu
from jax.sharding import PartitionSpec as P

NT = 32
FIRST_BIN = 2
LANES = 128
BLOCK = 16
MESH = pl.DeviceIdType.MESH


def repeat(count, body):
    if count <= 4:
        for step in range(count):
            body(step)
    else:

        def one(step, carry):
            body(step)
            return carry

        lax.fori_loop(0, count, one, 0)


def exchange_kernel(
    tiles,
    freqs,
    ranks,
    x_hbm,
    v_hbm,
    u_hbm,
    bounds_hbm,
    table_hbm,
    out,
    bounds_out,
    table_out,
    x_vm,
    v_vm,
    u_vm,
    own,
    held,
    u_turned,
    spec,
    load_sem,
    own_send,
    relay_send,
    coef_recv,
    spec_send,
    spec_recv,
    ready,
):
    rows = v_vm.shape[0]
    slots = v_vm.shape[2]
    owners = tiles // rows
    chunks = own.shape[0]
    receivers = u_vm.shape[3]
    quarter = receivers // freqs
    me = lax.axis_index("tile")
    my_freq = lax.axis_index("freq")
    my_row = me // owners
    first = my_row * owners
    last = first + owners - 1

    v_load = pltpu.make_async_copy(v_hbm.at[0, 0], v_vm, load_sem.at[0])
    u_load = pltpu.make_async_copy(u_hbm.at[0], u_vm, load_sem.at[1])
    bounds_load = pltpu.make_async_copy(bounds_hbm, bounds_out, load_sem.at[2 + chunks])
    table_load = pltpu.make_async_copy(table_hbm, table_out, load_sem.at[3 + chunks])
    x_loads = []
    for k in range(chunks):
        columns = pl.ds(k * LANES, LANES)
        x_loads.append(
            pltpu.make_async_copy(
                x_hbm.at[0, :, :, columns], x_vm.at[:, :, columns], load_sem.at[2 + k]
            )
        )
    barrier = pltpu.get_barrier_semaphore()
    def greet(semaphore, axis, place, size, way):
        for step in range(1, size):
            target = place + way * step

            @pl.when((target >= 0) & (target < size))
            def _(target=target):
                pl.semaphore_signal(
                    semaphore,
                    inc=1,
                    device_id={axis: jnp.clip(target, 0, size - 1)},
                    device_id_type=MESH,
                )

    greet(barrier, "tile", me, tiles, 1)
    greet(barrier, "freq", my_freq, freqs, 1)

    v_load.start()
    for load in x_loads:
        load.start()
    u_load.start()
    bounds_load.start()
    table_load.start()

    def own_copies(k, row):
        low = row * owners
        high = low + owners - 1

        def copy(target, way):
            return pltpu.make_async_remote_copy(
                src_ref=own.at[k, row],
                dst_ref=held.at[k, me],
                send_sem=own_send.at[k, row, way],
                recv_sem=coef_recv.at[k, me],
                device_id={"tile": target},
                device_id_type=MESH,
            )

        upward = copy(jnp.maximum(jnp.minimum(me + 1, tiles - 1), low), 0)
        downward = copy(jnp.minimum(jnp.maximum(me - 1, 0), high), 1)
        return (me < high, upward), (me > low, downward)

    def relay_copy(k, source):
        from_below = source < me
        wanted = jnp.where(from_below, me < last, me > first)
        target = jnp.where(from_below, jnp.minimum(me + 1, tiles - 1), jnp.maximum(me - 1, 0))
        copy = pltpu.make_async_remote_copy(
            src_ref=held.at[k, source],
            dst_ref=held.at[k, source],
            send_sem=relay_send.at[k, source],
            recv_sem=coef_recv.at[k, source],
            device_id={"tile": target},
            device_id_type=MESH,
        )
        return wanted, copy

    def arrival(step):
        below = me
        above = tiles - 1 - me
        below_first = jnp.where(step < below, me - 1 - step, step + 1)
        above_first = jnp.where(step < above, me + 1 + step, me - 1 - (step - above))
        return jnp.where((me - first) * 2 < owners, below_first, above_first)

    def spec_copy(k, step):
        target = lax.rem(my_freq + step, freqs)
        return pltpu.make_async_remote_copy(
            src_ref=spec.at[k, target],
            dst_ref=out.at[my_freq, :, :, pl.ds(k * LANES, LANES)],
            send_sem=spec_send.at[k, step],
            recv_sem=spec_recv.at[k, my_freq],
            device_id={"freq": target},
            device_id_type=MESH,
        )

    early = chunks
    order = sorted(range(freqs), key=lambda step: (step == 0, step != freqs // 2, step))

    def send(k, way):
        def send_row(row):
            wanted, copy = own_copies(k, row)[way]
            pl.when(wanted)(copy.start)

        repeat(rows, send_row)

    v_load.wait()
    slot_index = lax.broadcasted_iota(jnp.int32, (slots, 2 * LANES), 0)
    for k in range(chunks):
        x_loads[k].wait()
        columns = slice(k * LANES, (k + 1) * LANES)
        x_pair = jnp.concatenate([x_vm[0, :, columns], x_vm[1, :, columns]], axis=1)

        def make_row(row, k=k, x_pair=x_pair):
            products = jnp.dot(
                v_vm[row].reshape(2 * slots, v_vm.shape[3]),
                x_pair,
                preferred_element_type=jnp.float32,
            )
            real = products[:slots, :LANES] - products[slots:, LANES:]
            imag = products[:slots, LANES:] + products[slots:, :LANES]
            pair = jnp.concatenate([real, imag], axis=1)
            live = slot_index < ranks[row]
            own[k, row] = jnp.where(live, pair, 0.0).astype(jnp.bfloat16)

        repeat(rows, make_row)
        held[k, me] = own[k, my_row]
        if k == 0:

            @pl.when(me + my_freq > 0)
            def _():
                pl.semaphore_wait(barrier, me + my_freq)

            greet(ready.at[0], "tile", me, tiles, -1)
            greet(ready.at[1], "freq", my_freq, freqs, -1)
        send(k, 1)
        if k == early - 1:

            @pl.when(me < tiles - 1)
            def _():
                pl.semaphore_wait(ready.at[0], tiles - 1 - me)

            for earlier in range(early):
                send(earlier, 0)
        elif k >= early:
            send(k, 0)

    u_load.wait()
    for part in range(2):
        turned = u_vm[:, part].reshape(tiles * slots, receivers).T
        u_turned[:, pl.ds(part * quarter, quarter)] = turned.reshape(
            freqs, quarter, tiles * slots
        )

    @pl.when(my_freq < freqs - 1)
    def _():
        pl.semaphore_wait(ready.at[1], freqs - 1 - my_freq)

    for k in range(chunks):

        def take(step, k=k):
            source = arrival(step)
            wanted, copy = relay_copy(k, source)
            copy.wait_recv()
            pl.when(wanted)(copy.start)

        repeat(tiles - 1, take)
        coef = held[k].reshape(tiles * slots, 2 * LANES)
        for step in order:
            target = lax.rem(my_freq + step, freqs)
            products = jnp.dot(u_turned[target], coef, preferred_element_type=jnp.float32)
            real = products[:quarter, :LANES] - products[quarter:, LANES:]
            imag = products[:quarter, LANES:] + products[quarter:, :LANES]
            if step > 0:
                spec[k, target, 0] = real.astype(jnp.bfloat16)
                spec[k, target, 1] = imag.astype(jnp.bfloat16)
                spec_copy(k, step).start()
            else:
                columns = slice(k * LANES, (k + 1) * LANES)
                out[my_freq, 0, :, columns] = real.astype(jnp.bfloat16)
                out[my_freq, 1, :, columns] = imag.astype(jnp.bfloat16)

    bounds_load.wait()
    table_load.wait()
    for k in range(chunks):

        def drain_row(row, k=k):
            for wanted, copy in own_copies(k, row):
                pl.when(wanted)(copy.wait_send)

        repeat(rows, drain_row)

        def drain_relay(step, k=k):
            wanted, copy = relay_copy(k, arrival(step))
            pl.when(wanted)(copy.wait_send)

        repeat(tiles - 1, drain_relay)
        for step in range(1, freqs):
            spec_copy(k, step).wait_send()
    for k in range(chunks):
        for step in range(1, freqs):
            source = lax.rem(my_freq + step, freqs)
            pltpu.make_async_remote_copy(
                src_ref=spec.at[k, 0],
                dst_ref=out.at[source, :, :, pl.ds(k * LANES, LANES)],
                send_sem=spec_send.at[k, step],
                recv_sem=spec_recv.at[k, source],
                device_id={"freq": source},
                device_id_type=MESH,
            ).wait_recv()


def exchange(ranks, sources, v_factors, u_factors, bounds, table, tiles, freqs):
    rows, _, slots, edge = v_factors.shape[2:]
    receivers = u_factors.shape[4]
    width = sources.shape[3]
    chunks = width // LANES
    quarter = receivers // freqs
    bf16 = jnp.bfloat16
    dma = pltpu.SemaphoreType.DMA
    anywhere = pl.BlockSpec(memory_space=pl.ANY)
    within = pl.BlockSpec(memory_space=pltpu.VMEM)
    return pl.pallas_call(
        functools.partial(exchange_kernel, tiles, freqs),
        out_shape=(
            pltpu.VMEM((freqs, 2, quarter, width), bf16),
            pltpu.VMEM(bounds.shape, bounds.dtype),
            pltpu.VMEM(table.shape, table.dtype),
        ),
        in_specs=[pl.BlockSpec(memory_space=pltpu.SMEM)] + [anywhere] * 5,
        out_specs=(within, within, within),
        scratch_shapes=[
            pltpu.VMEM(sources.shape[1:], bf16),
            pltpu.VMEM((rows, 2, slots, edge), bf16),
            pltpu.VMEM((tiles, 2, slots, receivers), bf16),
            pltpu.VMEM((chunks, rows, slots, 2 * LANES), bf16),
            pltpu.VMEM((chunks, tiles, slots, 2 * LANES), bf16),
            pltpu.VMEM((freqs, 2 * quarter, tiles * slots), bf16),
            pltpu.VMEM((chunks, freqs, 2, quarter, LANES), bf16),
            dma((4 + chunks,)),
            dma((chunks, rows, 2)),
            dma((chunks, tiles)),
            dma((chunks, tiles)),
            dma((chunks, freqs)),
            dma((chunks, freqs)),
            pltpu.SemaphoreType.REGULAR((2,)),
        ],
        compiler_params=pltpu.CompilerParams(
            collective_id=0, has_side_effects=True, vmem_limit_bytes=56 * 2**20
        ),
        name="exchange",
    )(ranks.reshape(rows), sources, v_factors, u_factors, bounds, table)


def block_table(freqs, block):
    steps = (np.arange(freqs)[:, None] + FIRST_BIN) * np.arange(NT)[None, :] % NT
    angles = steps * (2.0 * math.pi / NT)
    table = np.stack([np.cos(angles), -np.sin(angles)], axis=1) / math.sqrt(freqs)
    whole = np.einsum("fcn,rq->rnfcq", table, np.eye(block))
    whole = whole.reshape(block * NT, freqs * 2 * block).astype(np.float32)
    high = whole.astype(ml_dtypes.bfloat16)
    low = (whole - high.astype(np.float32)).astype(ml_dtypes.bfloat16)
    return np.concatenate([high, low], axis=1)


def window_kernel(spec, bounds, table, out_hbm, out, store_sem):
    quarter, count, width = out.shape
    depth = table.shape[1] // 2
    half = table.shape[0] // count // 2
    pieces = quarter // (2 * half)
    time_index = lax.broadcasted_iota(jnp.int32, (half, count, width), 1)
    stores = []
    for piece in range(pieces):
        base = piece * 2 * half
        block = spec[:, :, base : base + 2 * half, :].reshape(depth, width)
        stacked = jnp.concatenate([block, block], axis=0)
        for side in range(2):
            part = slice(base + side * half, base + (side + 1) * half)
            weights = table[side * half * count : (side + 1) * half * count, :]
            traces = jnp.dot(weights, stacked, preferred_element_type=jnp.float32)
            traces = traces.reshape(half, count, width)
            lower = bounds[0, part, :][:, None, :]
            upper = bounds[1, part, :][:, None, :]
            inside = (time_index >= lower) & (time_index < upper)
            out[part] = jnp.where(inside, traces, 0.0)
            rows = pl.ds(base + side * half, half)
            store = pltpu.make_async_copy(
                out.at[rows], out_hbm.at[rows], store_sem.at[2 * piece + side]
            )
            store.start()
            stores.append(store)
    for store in stores:
        store.wait()


def transform(spectra, bounds, table):
    quarter, width = bounds.shape[1:]
    stores = 2 * quarter // BLOCK
    return pl.pallas_call(
        window_kernel,
        out_shape=jax.ShapeDtypeStruct((quarter, NT, width), jnp.float32),
        in_specs=[pl.BlockSpec(memory_space=pltpu.VMEM)] * 3,
        out_specs=pl.BlockSpec(memory_space=pl.ANY),
        scratch_shapes=[
            pltpu.VMEM((quarter, NT, width), jnp.float32),
            pltpu.SemaphoreType.DMA((stores,)),
        ],
        compiler_params=pltpu.CompilerParams(vmem_limit_bytes=24 * 2**20),
        name="transform",
    )(spectra, bounds, table)


def solution(mesh):
    tiles = mesh.shape["tile"]
    freqs = mesh.shape["freq"]

    def per_device(sources, v_factors, u_factors, tile_ranks, window_bounds):
        table = jnp.asarray(block_table(freqs, BLOCK))
        handed = exchange(
            tile_ranks, sources, v_factors, u_factors, window_bounds, table, tiles, freqs
        )
        return transform(*handed)

    return jax.shard_map(
        per_device,
        mesh=mesh,
        in_specs=(
            P("freq", "grp", "tile", None),
            P("freq", "tile", None, "grp", None, None),
            P("freq", None, "grp", None, "tile"),
            P("freq", "grp", "tile"),
            P("grp", ("tile", "freq"), None),
        ),
        out_specs=P(("tile", "freq"), "grp", None),
        check_vma=False,
    )
```
